256 devices in a mesh: section: 16 (over y_lo, z), tensor: 16 (over y_hi, x, core).
Axes of the slice: x: 4, y: 4 (y_hi: 2, y_lo: 2; y = y_hi * 2 + y_lo), z: 8, core: 2. Of those that a mesh axis runs over, the one named last changes fastest.
Arguments:
- encoder_states: bfloat16 [512, 5120], P('section', 'tensor'), may hold values from -6 to 6
- queries: bfloat16 [16, 128, 4096], P('section', None, 'tensor'), may hold values from -8 to 8
- grad_context: bfloat16 [16, 128, 4096], P('section', None, 'tensor'), may hold values from -6 to 6
- key_weight: bfloat16 [16, 5120, 4096], P('section', None, 'tensor'), may hold values from -0.078125 to 0.078125
- value_weight: bfloat16 [16, 5120, 4096], P('section', None, 'tensor'), may hold values from -0.078125 to 0.078125
Outputs:
- context: bfloat16 [16, 128, 4096], P('section', None, 'tensor')
- grad_queries: bfloat16 [16, 128, 4096], P('section', None, 'tensor')
- grad_key_weight: bfloat16 [16, 5120, 4096], P('section', None, 'tensor')
- grad_value_weight: bfloat16 [16, 5120, 4096], P('section', None, 'tensor')
- grad_encoder: bfloat16 [512, 5120], P('section', 'tensor')
The draws below stay inside these ranges and needn't reach their ends.
All inputs are finite; a program needn't handle non-finite values.
Results may differ from the reference program's by a relative error of at most 0.03.
Values may be sent and summed in bfloat16 or wider, within the bound.
A program may use at most 128 MiB of HBM per device.

```python
import jax
import jax.numpy as jnp
from jax import lax

D = 5120
HEADS = 32
HS = 128
SRC = 512
TGT = 128
SEQS = 1
LAYERS = 16
QTOK = 128
MTOK = 512


def block_levels(rng, dims, pieces, smallest, largest):
    loudness, own = 1.0, jax.random.fold_in(rng, 6)
    for position, parts in pieces:
        steps = jnp.exp(jax.random.uniform(jax.random.fold_in(own, position), (parts,), jnp.float32, smallest / len(pieces), largest / len(pieces)))
        loudness = loudness * jnp.repeat(steps, dims[position] // parts).reshape([-1 if axis == position else 1 for axis in range(len(dims))])
    return loudness


def noise(key, dims, scale, bound, split=(), kind=jnp.bfloat16):
    result = scale * jax.random.normal(key, dims, jnp.float32)
    if split:
        result = result * block_levels(key, dims, split, -0.22, 0.18)
    return jnp.clip(result, -bound, bound).astype(kind)


def setup_inputs(seed: int = 0) -> dict:
    key_of = jax.random.split(jax.random.key(seed), 6)
    return {
        "encoder_states": noise(key_of[0], (MTOK, D), 1.0, 6.0, ((0, 16), (1, 16))),
        "queries": noise(key_of[1], (LAYERS, QTOK, HEADS * HS), 2.0, 8.0, ((0, 16), (2, 16))),
        "grad_context": noise(key_of[2], (LAYERS, QTOK, HEADS * HS), 1.0, 6.0, ((0, 16), (2, 16))),
        "key_weight": noise(key_of[3], (LAYERS, D, HEADS * HS), D ** -0.5, 0.078125, ((0, 16), (2, 16))),
        "value_weight": noise(key_of[4], (LAYERS, D, HEADS * HS), D ** -0.5, 0.078125, ((0, 16), (2, 16))),
    }


soft_cap = 20.0


def attend(queries, keys, values, grad_context):
    scale = HS ** -0.5
    query4 = queries.astype(jnp.float32).reshape(SEQS, TGT, HEADS, HS)
    key4 = keys.astype(jnp.float32).reshape(SEQS, SRC, HEADS, HS)
    value4 = values.astype(jnp.float32).reshape(SEQS, SRC, HEADS, HS)
    grad4 = grad_context.astype(jnp.float32).reshape(SEQS, TGT, HEADS, HS)
    raw = jnp.einsum('sthd,skhd->shtk', query4, key4) * scale
    tangent = jnp.tanh(raw / soft_cap)
    weights = jnp.exp(soft_cap * tangent)
    probs = weights / jnp.sum(weights, axis=-1, keepdims=True)
    probs_low = probs.astype(jnp.bfloat16).astype(jnp.float32)
    context = jnp.einsum('shtk,skhd->sthd', probs_low, value4).astype(jnp.bfloat16)
    grad_probs = jnp.einsum('sthd,skhd->shtk', grad4, value4)
    grad_values = jnp.einsum('shtk,sthd->skhd', probs_low, grad4).astype(jnp.bfloat16)
    inner = jnp.sum(probs * grad_probs, axis=-1, keepdims=True)
    grad_raw = (probs * (grad_probs - inner) * (1.0 - tangent * tangent) * scale).astype(jnp.bfloat16).astype(jnp.float32)
    grad_queries = jnp.einsum('shtk,skhd->sthd', grad_raw, key4).astype(jnp.bfloat16)
    grad_keys = jnp.einsum('shtk,sthd->skhd', grad_raw, query4).astype(jnp.bfloat16)
    width = HEADS * HS
    return (context.reshape(QTOK, width), grad_queries.reshape(QTOK, width),
            grad_keys.reshape(MTOK, width), grad_values.reshape(MTOK, width))


def reference(encoder_states, queries, grad_context, key_weight, value_weight):
    def one_layer(grad_sum, layer):
        query_rows, grad_rows, key_mat, value_mat = layer
        keys = jnp.dot(encoder_states, key_mat, preferred_element_type=jnp.float32).astype(jnp.bfloat16)
        values = jnp.dot(encoder_states, value_mat, preferred_element_type=jnp.float32).astype(jnp.bfloat16)
        context, grad_q, grad_k, grad_v = attend(query_rows, keys, values, grad_rows)
        grad_kw = jnp.dot(encoder_states.T, grad_k, preferred_element_type=jnp.float32).astype(jnp.bfloat16)
        grad_vw = jnp.dot(encoder_states.T, grad_v, preferred_element_type=jnp.float32).astype(jnp.bfloat16)
        term = jnp.dot(grad_k, key_mat.T, preferred_element_type=jnp.float32)
        term = term + jnp.dot(grad_v, value_mat.T, preferred_element_type=jnp.float32)
        return grad_sum + term, (context, grad_q, grad_kw, grad_vw)

    start_sum = jnp.zeros((MTOK, D), jnp.float32)
    grad_sum, outputs = lax.scan(one_layer, start_sum, (queries, grad_context, key_weight, value_weight))
    context, grad_q, grad_kw, grad_vw = outputs
    return context, grad_q, grad_kw, grad_vw, grad_sum.astype(jnp.bfloat16)
```

```python
import functools

import jax
import jax.numpy as jnp
from jax import lax
from jax.experimental import pallas as pl
from jax.experimental.pallas import tpu as pltpu
from jax.sharding import PartitionSpec as P

MESH = pl.DeviceIdType.MESH
BF = jnp.bfloat16
F32 = jnp.float32

D = 5120
HS = 128
SRC = 512
TGT = 128
WIDE = 640
PART = WIDE // 2
CA = 256
CB = WIDE - CA
HALF = SRC // 2
UNIT = 16
SOFT_CAP = 20.0
SCALE = HS ** (-0.5)

EX = 0
A_PL = 1
A_Z = 17
B_Z = 31
B_P = 39
B_Q = 43
D_A = 59
D_B = 75
W_X = 91
G_X = 93
R_Q = 94
R_P = 110
R_Z = 114
S_Z = 122
S_PL = 136
FIN = 152
SLOTS = 153

NT = (((1,), (1,)), ((), ()))
TN = (((0,), (0,)), ((), ()))


def dot(a, b):
    return jnp.dot(a, b, preferred_element_type=F32)


def dot_nt(a, b):
    return lax.dot_general(a, b, NT, preferred_element_type=F32)


def dot_tn(a, b):
    return lax.dot_general(a, b, TN, preferred_element_type=F32)


def kernel(
    x_in, q_in, g_in, kw_in, vw_in,
    context, grad_q, grad_kw, grad_vw, grad_x,
    x, kw, vw, kwp, vwp, own_x, other_x, qv, gv,
    kacc, vacc, grads, grads_p, ts, recv_q, recv_p, recv_z, ring, plane, fin, fin_p,
    out_k, out_v,
    send_sem, recv_sem, local_sem, out_sem,
):
    s = lax.axis_index("section")
    t = lax.axis_index("tensor")
    y_lo, z = lax.div(s, 8), lax.rem(s, 8)
    y_hi, c = lax.div(t, 8), lax.rem(t, 2)
    px = lax.rem(lax.div(t, 2), 4)
    py = y_hi * 2 + y_lo
    block = y_hi * 4 + px

    def at(xx, yy, zz, cc):
        return (lax.rem(yy, 2) * 8 + zz, lax.div(yy, 2) * 8 + xx * 2 + cc)

    def shift(dx, dy):
        return lax.rem(px + dx + 4, 4), lax.rem(py + dy + 4, 4)

    def along(cc, dp, dq):
        return shift(dp * (1 - cc) + dq * cc, dp * cc + dq * (1 - cc))

    partner = at(px, py, z, 1 - c)

    def z_at(k):
        return lax.rem(z + k + 8, 8)

    def z_dev(k):
        return at(px, py, z_at(k), c)

    def rows16(cc, u, zz):
        return pl.ds(pl.multiple_of(cc * HALF + u * 128 + zz * UNIT, UNIT), UNIT)

    def remote(src, dst, slot, device):
        return pltpu.make_async_remote_copy(
            src_ref=src, dst_ref=dst, send_sem=send_sem.at[slot], recv_sem=recv_sem.at[slot],
            device_id=device, device_id_type=MESH,
        )

    sent = []

    def send(src, dst, slot, device):
        copy = remote(src, dst, slot, device)
        copy.start()
        sent.append(copy)

    def arrived(dst, slot):
        remote(dst, dst, slot, partner).wait_recv()

    rows_own = pl.ds(pl.multiple_of(c * UNIT, UNIT), UNIT)
    rows_other = pl.ds(pl.multiple_of((1 - c) * UNIT, UNIT), UNIT)
    loads = [
        pltpu.make_async_copy(x_in.at[rows_own], own_x, local_sem.at[0]),
        pltpu.make_async_copy(kw_in.at[0], kw, local_sem.at[1]),
        pltpu.make_async_copy(vw_in.at[0], vw, local_sem.at[2]),
        pltpu.make_async_copy(q_in.at[0], qv, local_sem.at[3]),
        pltpu.make_async_copy(g_in.at[0], gv, local_sem.at[4]),
    ]
    for load in loads:
        load.start()

    barrier = pltpu.get_barrier_semaphore()
    plane_offsets = [(dx, dy) for dy in range(4) for dx in range(4) if dx or dy]
    peers = [partner]
    peers += [z_dev(k) for k in range(1, 8)]
    peers += [at(*shift(dx, dy), z, c) for dx, dy in plane_offsets]
    for peer in peers:
        pl.semaphore_signal(barrier, inc=1, device_id=peer, device_id_type=MESH)
    pl.semaphore_wait(barrier, len(peers))

    send(x_in.at[rows_other], other_x, EX, partner)
    loads[0].wait()
    arrived(other_x, EX)
    mine, theirs = own_x[...].astype(F32), other_x[...].astype(F32)
    first = jnp.where(c == 0, mine, theirs)
    second = jnp.where(c == 0, theirs, mine)
    x[block, rows16(c, y_lo, z), :] = jnp.concatenate([first, second], axis=1).astype(BF)

    def a_unit(ref, xx, yy):
        return ref.at[lax.div(yy, 2) * 4 + xx, rows16(c, lax.rem(yy, 2), z), pl.ds(0, CA)]

    def a_chunk(ref, cc, u, zz):
        return ref.at[:, rows16(cc, u, zz), pl.ds(0, CA)]

    def b_unit(zz):
        return x.at[block, rows16(c, y_lo, zz), pl.ds(CA, CB)]

    def b_block(ref, cc, base, place):
        xx, yy = place
        rows = pl.ds(pl.multiple_of(base + lax.rem(yy, 2) * 128, 128), 128)
        return ref.at[lax.div(yy, 2) * 4 + xx, rows, pl.ds(CA, CB)]

    for k in range(1, 8):
        send(b_unit(z), b_unit(z), B_Z + k, z_dev(k))
    for dx, dy in plane_offsets:
        unit = a_unit(x, px, py)
        send(unit, unit, A_PL + dy * 4 + dx, at(*shift(dx, dy), z, c))

    def share_a(k, u):
        part = a_chunk(x, c, u, z_at(k))
        send(part, part, D_A + (k % 8) * 2 + u, partner)

    def share_b(j, k):
        part = b_block(x, c, c * HALF, along(c, -j, -k))
        send(part, part, D_B + j * 4 + k, partner)

    def spread_b(j):
        part = b_block(x, c, c * HALF, along(c, -j, 0))
        for k in range(1, 4):
            send(part, part, B_Q + j * 4 + k, at(*along(c, 0, k), z, c))
        share_b(j, 0)

    def pass_on(direction, index):
        sign = 1 - 2 * direction
        u = direction if index == 6 else index % 2
        part = a_chunk(x, c, u, z_at(-sign * (index // 2)))
        send(part, part, A_Z + direction * 7 + index, z_dev(sign))

    def ring_arrived(direction, index):
        sign = 1 - 2 * direction
        u = direction if index == 6 else index % 2
        k = -sign * (index // 2 + 1)
        arrived(a_chunk(x, c, u, z_at(k)), A_Z + direction * 7 + index)
        if index + 2 < 6 or (index + 2 == 6 and direction == 0) or (index == 5 and direction == 1):
            pass_on(direction, min(index + 2, 6))
        share_a(k, u)

    for k in range(1, 8):
        arrived(b_unit(z_at(-k)), B_Z + k)
    own_block = b_block(x, c, c * HALF, along(c, 0, 0))
    for k in range(1, 4):
        send(own_block, own_block, B_P + k, at(*along(c, k, 0), z, c))
    spread_b(0)

    for dx, dy in plane_offsets:
        arrived(a_unit(x, *shift(-dx, -dy)), A_PL + dy * 4 + dx)
    for index in range(2):
        pass_on(0, index)
        pass_on(1, index)
    send(kw_in.at[0], kwp, W_X, partner)
    send(vw_in.at[0], vwp, W_X + 1, partner)
    share_a(0, 0)
    share_a(0, 1)

    for j in range(1, 4):
        arrived(b_block(x, c, c * HALF, along(c, -j, 0)), B_P + j)
        spread_b(j)
        if j < 3:
            for index in (2 * j - 2, 2 * j - 1):
                ring_arrived(0, index)
                ring_arrived(1, index)
    for index in (4, 5, 6):
        ring_arrived(0, index)
        ring_arrived(1, index)
        j = index - 4
        for k in range(1, 4):
            arrived(b_block(x, c, c * HALF, along(c, -j, -k)), B_Q + j * 4 + k)
            share_b(j, k)
    for k in range(1, 4):
        arrived(b_block(x, c, c * HALF, along(c, -3, -k)), B_Q + 12 + k)
        share_b(3, k)

    for k in range(8):
        for u in range(2):
            arrived(a_chunk(x, 1 - c, u, z_at(k)), D_A + k * 2 + u)
    for j in range(4):
        for k in range(4):
            arrived(b_block(x, 1 - c, (1 - c) * HALF, along(1 - c, -j, -k)), D_B + j * 4 + k)

    loads[1].wait()
    loads[2].wait()
    for i in range(4):
        wide = jnp.concatenate([x[2 * i], x[2 * i + 1]], axis=1)
        rows = pl.ds(i * 2 * WIDE, 2 * WIDE)
        k_part, v_part = dot(wide, kw[rows, :]), dot(wide, vw[rows, :])
        if i == 0:
            kacc[...], vacc[...] = k_part, v_part
        else:
            kacc[...] += k_part
            vacc[...] += v_part

    loads[3].wait()
    loads[4].wait()
    for head in range(2):
        cols = pl.ds(head * HS, HS)
        query, grad = qv[:, cols], gv[:, cols]
        key, value = kacc[:, cols].astype(BF), vacc[:, cols].astype(BF)
        tangent = jnp.tanh(dot_nt(query, key) * SCALE / SOFT_CAP)
        weights = jnp.exp(SOFT_CAP * tangent)
        probs = weights / jnp.sum(weights, axis=-1, keepdims=True)
        probs_low = probs.astype(BF)
        context[0, :, cols] = dot(probs_low, value).astype(BF)
        grad_probs = dot_nt(grad, value)
        inner = jnp.sum(probs * grad_probs, axis=-1, keepdims=True)
        grad_raw = (probs * (grad_probs - inner) * (1.0 - tangent * tangent) * SCALE).astype(BF)
        grad_q[0, :, cols] = dot(grad_raw, key).astype(BF)
        grads[:, cols] = dot_tn(grad_raw, query).astype(BF)
        grads[:, pl.ds(2 * HS + head * HS, HS)] = dot_tn(probs_low, grad).astype(BF)

    rows_p = pl.ds(pl.multiple_of((1 - c) * HALF, HALF), HALF)
    rows_c = pl.ds(pl.multiple_of(c * HALF, HALF), HALF)
    send(grads.at[rows_p], grads_p, G_X, partner)

    pieces = [(i, out) for i in range(4) for out in range(2)]
    stores = []

    def weight_grad():
        i, out = pieces.pop(0)
        rows = pl.ds(i * 2 * WIDE, 2 * WIDE)
        held, target = ((out_k, grad_kw), (out_v, grad_vw))[out]
        wide = jnp.concatenate([x[2 * i], x[2 * i + 1]], axis=1)
        held[rows, :] = dot_tn(wide, grads[:, pl.ds(out * 256, 256)]).astype(BF)
        store = pltpu.make_async_copy(held.at[rows], target.at[0, rows], out_sem.at[i * 2 + out])
        store.start()
        stores.append(store)

    weight_grad()
    arrived(grads_p, G_X)
    arrived(kwp, W_X)
    arrived(vwp, W_X + 1)

    def term(row_base, rows, feature, width):
        mine = pl.ds(pl.multiple_of(c * HALF + row_base, 128), rows)
        theirs = pl.ds(pl.multiple_of(row_base, 128), rows)
        span = pl.ds(pl.multiple_of(feature, 128), width)
        return (
            dot_nt(grads[mine, 0:256], kw[span, :])
            + dot_nt(grads[mine, 256:512], vw[span, :])
            + dot_nt(grads_p[theirs, 0:256], kwp[span, :])
            + dot_nt(grads_p[theirs, 256:512], vwp[span, :])
        ).astype(BF)

    for i in range(8):
        ts[i, :, 0:CA] = term(0, HALF, i * WIDE, CA)

    def t_chunk(u, zz):
        return a_chunk(ts, 0, u, zz)

    def scatter(direction, index):
        sign = 1 - 2 * direction
        u = direction if index == 0 else (index - 1) % 2 ^ direction
        part = t_chunk(u, z_at(sign * (4 - (index + 1) // 2)))
        send(part, ring.at[direction * 7 + index], S_Z + direction * 7 + index, z_dev(sign))

    def add(direction, index):
        sign = 1 - 2 * direction
        u = direction if index == 0 else (index - 1) % 2 ^ direction
        held = ring.at[direction * 7 + index]
        arrived(held, S_Z + direction * 7 + index)
        rows = rows16(0, u, z_at(sign * (3 - (index + 1) // 2)))
        ts[:, rows, 0:CA] = (ts[:, rows, 0:CA].astype(F32) + held[...].astype(F32)).astype(BF)
        if index < 5:
            scatter(direction, 1 if index == 0 else index + 2)

    for index in (0, 2):
        scatter(0, index)
        scatter(1, index)

    def compute_b(j, k):
        xx, yy = along(c, j, k)
        low = lax.rem(yy, 2) * 128
        chip = lax.div(yy, 2) * 4 + xx
        rows = pl.ds(pl.multiple_of(low, 128), 128)
        ts[chip, rows, CA:WIDE] = term(low, 128, chip * WIDE + CA, CB)

    def send_b(j, k):
        send(
            b_block(ts, c, 0, along(c, j, k)), recv_q.at[j * 3 + k - 1],
            R_Q + j * 4 + k, at(*along(c, 0, k), z, c),
        )

    for j in (1, 2, 3, 0):
        for k in range(1, 4):
            compute_b(j, k)
            send_b(j, k)
        if j == 2:
            add(0, 0)
            add(1, 0)
    for j in (1, 2, 3, 0):
        compute_b(j, 0)

    def sum_b(j):
        xx, yy = along(c, j, 0)
        rows = pl.ds(pl.multiple_of(lax.rem(yy, 2) * 128, 128), 128)
        chip = lax.div(yy, 2) * 4 + xx
        total = ts[chip, rows, CA:WIDE].astype(F32)
        for k in range(1, 4):
            arrived(recv_q.at[j * 3 + k - 1], R_Q + j * 4 + k)
            total = total + recv_q[j * 3 + k - 1].astype(F32)
        ts[chip, rows, CA:WIDE] = total.astype(BF)

    weight_grad()
    for index in (1, 2):
        add(0, index)
        add(1, index)
    weight_grad()
    for index in (3, 4):
        add(0, index)
        add(1, index)
    weight_grad()
    for j in (1, 2, 3):
        sum_b(j)
        send(
            b_block(ts, c, 0, along(c, j, 0)), recv_p.at[j - 1], R_P + j, at(*along(c, j, 0), z, c)
        )
    sum_b(0)
    for index in (5, 6):
        add(0, index)
        add(1, index)
    for dx, dy in plane_offsets:
        xx, yy = shift(dx, dy)
        send(
            a_unit_t(ts, xx, yy, z), plane.at[dy * 4 + dx], S_PL + dy * 4 + dx, at(xx, yy, z, c)
        )
    weight_grad()

    rows_b = pl.ds(pl.multiple_of(y_lo * 128, 128), 128)
    total = ts[block, rows_b, CA:WIDE].astype(F32)
    for j in range(1, 4):
        arrived(recv_p.at[j - 1], R_P + j)
        total = total + recv_p[j - 1].astype(F32)
    ts[block, rows_b, CA:WIDE] = total.astype(BF)
    for k in range(1, 8):
        part = ts.at[block, rows16(0, y_lo, z_at(k)), pl.ds(CA, CB)]
        send(part, recv_z.at[k - 1], R_Z + k, z_dev(k))
    weight_grad()

    rows_own = rows16(0, y_lo, z)
    total = ts[block, rows_own, 0:CA].astype(F32)
    for dx, dy in plane_offsets:
        arrived(plane.at[dy * 4 + dx], S_PL + dy * 4 + dx)
        total = total + plane[dy * 4 + dx].astype(F32)
    fin[:, 0:CA] = total.astype(BF)
    weight_grad()
    total = ts[block, rows_own, CA:WIDE].astype(F32)
    for k in range(1, 8):
        arrived(recv_z.at[k - 1], R_Z + k)
        total = total + recv_z[k - 1].astype(F32)
    fin[:, CA:WIDE] = total.astype(BF)
    send(fin, fin_p, FIN, partner)
    weight_grad()
    arrived(fin_p, FIN)
    mine, theirs = fin[...].astype(F32), fin_p[...].astype(F32)
    whole = jnp.concatenate(
        [jnp.where(c == 0, mine, theirs), jnp.where(c == 0, theirs, mine)], axis=0
    )
    grad_x[...] = jnp.where(c == 0, whole[:, 0:PART], whole[:, PART:WIDE]).astype(BF)

    for copy in sent:
        copy.wait_send()
    for store in stores:
        store.wait()


def a_unit_t(ref, xx, yy, zz):
    row = pl.multiple_of(lax.rem(yy, 2) * 128 + zz * UNIT, UNIT)
    return ref.at[lax.div(yy, 2) * 4 + xx, pl.ds(row, UNIT), pl.ds(0, CA)]


def per_device(encoder_states, queries, grad_context, key_weight, value_weight):
    anywhere = pl.BlockSpec(memory_space=pl.ANY)
    vmem = pl.BlockSpec(memory_space=pltpu.VMEM)
    shape = jax.ShapeDtypeStruct
    return pl.pallas_call(
        kernel,
        out_shape=(
            shape((1, TGT, 256), BF),
            shape((1, TGT, 256), BF),
            shape((1, D, 256), BF),
            shape((1, D, 256), BF),
            shape((32, PART), BF),
        ),
        in_specs=[anywhere] * 5,
        out_specs=(vmem, vmem, anywhere, anywhere, vmem),
        scratch_shapes=[
            pltpu.VMEM((8, SRC, WIDE), BF),
            pltpu.VMEM((D, 256), BF),
            pltpu.VMEM((D, 256), BF),
            pltpu.VMEM((D, 256), BF),
            pltpu.VMEM((D, 256), BF),
            pltpu.VMEM((UNIT, PART), BF),
            pltpu.VMEM((UNIT, PART), BF),
            pltpu.VMEM((TGT, 256), BF),
            pltpu.VMEM((TGT, 256), BF),
            pltpu.VMEM((SRC, 256), F32),
            pltpu.VMEM((SRC, 256), F32),
            pltpu.VMEM((SRC, 512), BF),
            pltpu.VMEM((HALF, 512), BF),
            pltpu.VMEM((8, HALF, WIDE), BF),
            pltpu.VMEM((12, 128, CB), BF),
            pltpu.VMEM((3, 128, CB), BF),
            pltpu.VMEM((7, UNIT, CB), BF),
            pltpu.VMEM((14, 8, UNIT, CA), BF),
            pltpu.VMEM((16, UNIT, CA), BF),
            pltpu.VMEM((UNIT, WIDE), BF),
            pltpu.VMEM((UNIT, WIDE), BF),
            pltpu.VMEM((D, 256), BF),
            pltpu.VMEM((D, 256), BF),
            pltpu.SemaphoreType.DMA((SLOTS,)),
            pltpu.SemaphoreType.DMA((SLOTS,)),
            pltpu.SemaphoreType.DMA((5,)),
            pltpu.SemaphoreType.DMA((8,)),
        ],
        compiler_params=pltpu.CompilerParams(
            collective_id=0, has_side_effects=True, vmem_limit_bytes=56 << 20
        ),
        cost_estimate=pl.CostEstimate(
            flops=8_500_000_000, bytes_accessed=11_000_000, transcendentals=262_144
        ),
        name="cross_attention_step",
    )(encoder_states, queries, grad_context, key_weight, value_weight)


def solution(mesh):
    in_specs = (
        P("section", "tensor"),
        P("section", None, "tensor"),
        P("section", None, "tensor"),
        P("section", None, "tensor"),
        P("section", None, "tensor"),
    )
    out_specs = (
        P("section", None, "tensor"),
        P("section", None, "tensor"),
        P("section", None, "tensor"),
        P("section", None, "tensor"),
        P("section", "tensor"),
    )
    return jax.shard_map(
        per_device, mesh=mesh, in_specs=in_specs, out_specs=out_specs, check_vma=False
    )
```

```python
import functools

import jax
import jax.numpy as jnp
from jax import lax
from jax.experimental import pallas as pl
from jax.experimental.pallas import tpu as pltpu
from jax.sharding import PartitionSpec as P

MESH = pl.DeviceIdType.MESH
BF = jnp.bfloat16
F32 = jnp.float32

D = 5120
HS = 128
SRC = 512
TGT = 128
WIDE = 640
PART = WIDE // 2
CA = 256
CB = WIDE - CA
HALF = SRC // 2
UNIT = 16
SOFT_CAP = 20.0
SCALE = HS ** (-0.5)

EX = 0
A_PL = 1
A_Z = 5
B_Z = 33
B_P = 34
B_Q = 38
SHARE = 42
W_X = 43
G_X = 44
R_Q = 45
R_P = 49
R_Z = 50
S_Z = 51
S_PL = 83
FIN = 84
RECEIVES = 85

OUT_EX, OUT_UNIT, OUT_ROW, OUT_TILE, OUT_BLOCK, OUT_W, OUT_G, OUT_SUM, OUT_TERM, OUT_FIN = range(10)
SENDS = 10

RING_A = ((3, 0), (3, 1), (2, 2), (2, 3), (2, 0), (2, 1), (1, 2), (1, 3), (1, 0), (1, 1), (0, 2), (0, 3), (0, 0), (0, 1))
RING_B = ((2, 0), (2, 1), (3, 2), (3, 3), (1, 0), (1, 1), (2, 2), (2, 3), (0, 0), (0, 1), (1, 2), (1, 3), (0, 2), (0, 3))

NT = (((1,), (1,)), ((), ()))
TN = (((0,), (0,)), ((), ()))


def dot(a, b):
    return jnp.dot(a, b, preferred_element_type=F32)


def dot_nt(a, b):
    return lax.dot_general(a, b, NT, preferred_element_type=F32)


def dot_tn(a, b):
    return lax.dot_general(a, b, TN, preferred_element_type=F32)


def kernel(
    x_in, q_in, g_in, kw_in, vw_in,
    context, grad_q, grad_kw, grad_vw, grad_x,
    x, kw, vw, pair_w, own_x, other_x, qv, gv,
    keys, values, grads, grads_p, ts, recv_q, recv_p, recv_z, ring, plane, fin, fin_p,
    send_sem, recv_sem, local_sem,
):
    s = lax.axis_index("section")
    t = lax.axis_index("tensor")
    y_lo, z = lax.div(s, 8), lax.rem(s, 8)
    y_hi, c = lax.div(t, 8), lax.rem(t, 2)
    px = lax.rem(lax.div(t, 2), 4)
    py = y_hi * 2 + y_lo
    block = y_hi * 4 + px

    def at(xx, yy, zz, cc):
        return (lax.rem(yy, 2) * 8 + zz, lax.div(yy, 2) * 8 + xx * 2 + cc)

    def along(cc, dp, dq):
        dx = dp * (1 - cc) + dq * cc
        high = abs(dq) // 2 * (1 - cc) + abs(dp) // 2 * cc
        low = abs(dq) % 2 * (1 - cc) + abs(dp) % 2 * cc
        yy = (y_hi + high - 2 * y_hi * high) * 2 + y_lo + low - 2 * y_lo * low
        return lax.rem(px + dx + 4, 4), yy

    partner = at(px, py, z, 1 - c)

    def z_at(k):
        return lax.rem(z + k + 8, 8)

    def z_dev(k):
        return at(px, py, z_at(k), c)

    def rows16(cc, u, zz):
        return pl.ds(pl.multiple_of(cc * HALF + u * 128 + zz * UNIT, UNIT), UNIT)

    def remote(src, dst, out, slot, device):
        return pltpu.make_async_remote_copy(
            src_ref=src, dst_ref=dst, send_sem=send_sem.at[out], recv_sem=recv_sem.at[slot],
            device_id=device, device_id_type=MESH,
        )

    def send(src, dst, out, slot, device):
        remote(src, dst, out, slot, device).start()

    def arrived(dst, slot):
        remote(dst, dst, OUT_EX, slot, partner).wait_recv()

    def left(src, out):
        remote(src, src, out, EX, partner).wait_send()

    rows_own = pl.ds(pl.multiple_of(c * UNIT, UNIT), UNIT)
    rows_other = pl.ds(pl.multiple_of((1 - c) * UNIT, UNIT), UNIT)
    loads = [
        pltpu.make_async_copy(x_in.at[rows_own], own_x, local_sem.at[0]),
        pltpu.make_async_copy(kw_in.at[0], kw, local_sem.at[1]),
        pltpu.make_async_copy(vw_in.at[0], vw, local_sem.at[2]),
        pltpu.make_async_copy(q_in.at[0], qv, local_sem.at[3]),
        pltpu.make_async_copy(g_in.at[0], gv, local_sem.at[4]),
    ]
    for load in loads:
        load.start()

    def row_of(m):
        return (1 - y_hi if m // 2 else y_hi), (1 - y_lo if m % 2 else y_lo)

    def in_plane(dx, m):
        high, low = row_of(m)
        return lax.rem(px + dx + 4, 4), high * 2 + low

    plane_offsets = [(dx, m) for m in (0, 1, 3, 2) for dx in (1, 3, 2, 0) if dx or m]

    barrier = pltpu.get_barrier_semaphore()
    peers = [z_dev(k) for k in (4, 3, 5, 2, 6, 1, 7)]
    peers += [at(*in_plane(dx, m), z, c) for dx, m in reversed(plane_offsets)]
    peers += [partner]
    for peer in peers:
        pl.semaphore_signal(barrier, inc=1, device_id=peer, device_id_type=MESH)
    pl.semaphore_wait(barrier, len(peers))

    send(x_in.at[rows_other], other_x, OUT_EX, EX, partner)
    loads[0].wait()
    arrived(other_x, EX)
    mine, theirs = own_x[...].astype(F32), other_x[...].astype(F32)
    first = jnp.where(c == 0, mine, theirs)
    second = jnp.where(c == 0, theirs, mine)
    x[block, rows16(c, y_lo, z), :] = jnp.concatenate([first, second], axis=1).astype(BF)

    def a_unit(ref, cc, place, zz):
        xx, yy = place
        return ref.at[lax.div(yy, 2) * 4 + xx, rows16(cc, lax.rem(yy, 2), zz), pl.ds(0, CA)]

    def a_row(ref, cc, m, zz):
        high, low = row_of(m)
        return ref.at[pl.ds(high * 4, 4), rows16(cc, low, zz), pl.ds(0, CA)]

    def b_unit(zz):
        return x.at[block, rows16(c, y_lo, zz), pl.ds(CA, CB)]

    def b_block(ref, cc, base, place):
        xx, yy = place
        rows = pl.ds(pl.multiple_of(base + lax.rem(yy, 2) * 128, 128), 128)
        return ref.at[lax.div(yy, 2) * 4 + xx, rows, pl.ds(CA, CB)]

    for dx, m in plane_offsets:
        unit = a_unit(x, c, (px, py), z)
        send(unit, unit, OUT_UNIT, A_PL + m, at(*in_plane(dx, m), z, c))
    for k in (1, 7, 2, 6, 3, 5, 4):
        send(b_unit(z), b_unit(z), OUT_TILE, B_Z, z_dev(k))

    def share_a(k, m):
        part = a_row(x, c, m, z_at(k))
        send(part, part, OUT_ROW, SHARE, partner)

    def share_b(j, k):
        part = b_block(x, c, c * HALF, along(c, -j, -k))
        send(part, part, OUT_BLOCK, SHARE, partner)

    def spread_b(j):
        part = b_block(x, c, c * HALF, along(c, -j, 0))
        for k in (1, 3, 2):
            send(part, part, OUT_BLOCK, B_Q + j, at(*along(c, 0, k), z, c))
        share_b(j, 0)

    def ring_slot(direction, step, m):
        return A_Z + direction * 14 + step * 4 + (m if step < 3 else m % 2)

    def pass_on(direction, step, m):
        sign = 1 - 2 * direction
        part = a_row(x, c, m, z_at(-sign * step))
        send(part, part, OUT_ROW, ring_slot(direction, step, m), z_dev(sign))

    def ring_arrived(step, m):
        for direction in range(2):
            if step == 3 and m // 2 != direction:
                continue
            k = -(1 - 2 * direction) * (step + 1)
            arrived(a_row(x, c, m, z_at(k)), ring_slot(direction, step, m))
            if step < 2 or (step == 2 and m // 2 == direction):
                pass_on(direction, step + 1, m)
            share_a(k, m)

    def ring_start(m):
        high, low = row_of(m)
        units = x.at[pl.ds(high * 4, 4 if m else 3), rows16(c, low, z), pl.ds(0, CA)]
        arrived(units, A_PL + m)
        pass_on(0, 0, m)
        pass_on(1, 0, m)
        share_a(0, m)

    ring_start(0)
    ring_start(1)
    arrived(x.at[block, pl.ds(0, 7 * UNIT), pl.ds(CA, CB)], B_Z)
    own_block = b_block(x, c, c * HALF, along(c, 0, 0))
    for k in (1, 3, 2):
        send(own_block, own_block, OUT_BLOCK, B_P + k, at(*along(c, k, 0), z, c))
    ring_start(3)
    ring_start(2)

    def block_arrived(j):
        arrived(b_block(x, c, c * HALF, along(c, -j, 0)), B_P + j)
        spread_b(j)

    def column_arrived(j):
        arrived(x.at[0:3, pl.ds(0, 128), pl.ds(CA, CB)], B_Q + j)
        for k in (1, 3, 2):
            share_b(j, k)

    ring_arrived(0, 0)
    ring_arrived(0, 1)
    spread_b(0)
    ring_arrived(0, 3)
    ring_arrived(0, 2)
    block_arrived(1)
    block_arrived(3)
    ring_arrived(1, 0)
    ring_arrived(1, 1)
    block_arrived(2)
    send(kw_in.at[0], pair_w.at[0], OUT_W, W_X, partner)
    send(vw_in.at[0], pair_w.at[1], OUT_W, W_X, partner)
    ring_arrived(1, 3)
    ring_arrived(1, 2)
    column_arrived(0)
    ring_arrived(2, 0)
    ring_arrived(2, 1)
    column_arrived(1)
    ring_arrived(2, 3)
    ring_arrived(2, 2)
    column_arrived(3)
    for m in (0, 1, 3, 2):
        ring_arrived(3, m)
    column_arrived(2)

    rows_c = pl.ds(pl.multiple_of(c * HALF, HALF), HALF)
    rows_p = pl.ds(pl.multiple_of((1 - c) * HALF, HALF), HALF)

    def project(rows):
        k_sum, v_sum = 0.0, 0.0
        for i in range(4):
            wide = jnp.concatenate([x[2 * i, rows, :], x[2 * i + 1, rows, :]], axis=1)
            span = pl.ds(i * 2 * WIDE, 2 * WIDE)
            k_sum += dot(wide, kw[span, :])
            v_sum += dot(wide, vw[span, :])
        keys[rows, :] = k_sum.astype(BF)
        values[rows, :] = v_sum.astype(BF)

    loads[1].wait()
    loads[2].wait()
    project(rows_c)
    arrived(x.at[:, rows_p, :], SHARE)
    project(rows_p)

    loads[3].wait()
    loads[4].wait()
    for head in range(2):
        cols = pl.ds(head * HS, HS)
        query, grad = qv[:, cols], gv[:, cols]
        key, value = keys[:, cols], values[:, cols]
        tangent = jnp.tanh(dot_nt(query, key) * SCALE / SOFT_CAP)
        weights = jnp.exp(SOFT_CAP * tangent)
        probs = weights / jnp.sum(weights, axis=-1, keepdims=True)
        probs_low = probs.astype(BF)
        context[0, :, cols] = dot(probs_low, value).astype(BF)
        grad_probs = dot_nt(grad, value)
        inner = jnp.sum(probs * grad_probs, axis=-1, keepdims=True)
        grad_raw = (probs * (grad_probs - inner) * (1.0 - tangent * tangent) * SCALE).astype(BF)
        grad_q[0, :, cols] = dot(grad_raw, key).astype(BF)
        grads[:, cols] = dot_tn(grad_raw, query).astype(BF)
        grads[:, pl.ds(2 * HS + head * HS, HS)] = dot_tn(probs_low, grad).astype(BF)

    send(grads.at[rows_p], grads_p, OUT_G, G_X, partner)

    pieces = [(i, out) for i in range(4) for out in range(2)]

    def weight_grad():
        i, out = pieces.pop(0)
        rows = pl.ds(i * 2 * WIDE, 2 * WIDE)
        wide = jnp.concatenate([x[2 * i], x[2 * i + 1]], axis=1)
        target = (grad_kw, grad_vw)[out]
        target[0, rows, :] = dot_tn(wide, grads[:, pl.ds(out * 256, 256)]).astype(BF)

    weight_grad()
    weight_grad()
    arrived(grads_p, G_X)
    arrived(pair_w, W_X)

    def term(feature, width):
        span = pl.ds(pl.multiple_of(feature, 128), width)
        return (
            dot_nt(grads[rows_c, 0:256], kw[span, :])
            + dot_nt(grads[rows_c, 256:512], vw[span, :])
            + dot_nt(grads_p[:, 0:256], pair_w[0, span, :])
            + dot_nt(grads_p[:, 256:512], pair_w[1, span, :])
        ).astype(BF)

    def compute_a(half):
        high = row_of(half * 2)[0]
        for i in range(4):
            chip = high * 4 + i
            ts[chip, :, 0:CA] = term(chip * WIDE, CA)

    def scatter(direction, togo, m):
        sign = 1 - 2 * direction
        index = direction * 16 + (togo - 1) * 4 + m
        send(a_row(ts, 0, m, z_at(sign * togo)), ring.at[index], OUT_SUM, S_Z + index, z_dev(sign))

    def add(direction, togo, m):
        sign = 1 - 2 * direction
        index = direction * 16 + togo * 4 + m
        held = ring.at[index]
        arrived(held, S_Z + index)
        high, low = row_of(m)
        chips, rows = pl.ds(high * 4, 4), rows16(0, low, z_at(sign * togo))
        ts[chips, rows, 0:CA] = (ts[chips, rows, 0:CA].astype(F32) + held[...].astype(F32)).astype(BF)
        if togo:
            scatter(direction, togo, m)

    def ring_event(*steps):
        for step in steps:
            add(0, *RING_A[step])
            add(1, *RING_B[step])

    def send_b(j):
        for k in (1, 3, 2):
            send(
                b_block(ts, c, 0, along(c, j, k)), recv_q.at[j, k - 1],
                OUT_TERM, R_Q + j, at(*along(c, 0, k), z, c),
            )

    def sum_b(j):
        xx, yy = along(c, j, 0)
        rows = pl.ds(pl.multiple_of(lax.rem(yy, 2) * 128, 128), 128)
        chip = lax.div(yy, 2) * 4 + xx
        total = ts[chip, rows, CA:WIDE].astype(F32)
        arrived(recv_q.at[j], R_Q + j)
        for k in range(3):
            total = total + recv_q[j, k].astype(F32)
        ts[chip, rows, CA:WIDE] = total.astype(BF)
        if j:
            part = b_block(ts, c, 0, along(c, j, 0))
            send(part, recv_p.at[j - 1], OUT_TERM, R_P, at(*along(c, j, 0), z, c))

    for chip in range(8):
        ts[chip, :, CA:WIDE] = term(chip * WIDE + CA, CB)
    for j in (1, 3, 2, 0):
        send_b(j)
    compute_a(0)
    for m in (0, 1):
        scatter(0, 4, m)
        scatter(1, 3, m)
    compute_a(1)
    for m in (2, 3):
        scatter(0, 3, m)
        scatter(1, 4, m)
    weight_grad()
    ring_event(0, 1, 2, 3)
    sum_b(1)
    ring_event(4, 5)
    sum_b(3)
    ring_event(6, 7)
    sum_b(2)
    ring_event(8, 9)
    sum_b(0)

    def send_plane(m):
        for dx in (2, 1, 3, 0):
            if dx or m:
                place = in_plane(dx, m)
                send(
                    a_unit(ts, 0, place, z), plane.at[m * 4 + dx - 1],
                    OUT_UNIT, S_PL, at(*place, z, c),
                )

    ring_event(10, 11, 12)
    send_plane(2)
    send_plane(0)
    ring_event(13)
    send_plane(3)
    send_plane(1)
    rows_b = pl.ds(pl.multiple_of(y_lo * 128, 128), 128)
    total = ts[block, rows_b, CA:WIDE].astype(F32)
    arrived(recv_p, R_P)
    for j in range(3):
        total = total + recv_p[j].astype(F32)
    ts[block, rows_b, CA:WIDE] = total.astype(BF)
    for k in (4, 3, 5, 2, 6, 1, 7):
        part = ts.at[block, rows16(0, y_lo, z_at(k)), pl.ds(CA, CB)]
        send(part, recv_z.at[k - 1], OUT_TILE, R_Z, z_dev(k))
    weight_grad()
    weight_grad()
    weight_grad()

    rows_own = rows16(0, y_lo, z)
    total = ts[block, rows_own, 0:CA].astype(F32)
    arrived(plane, S_PL)
    for index in range(15):
        total = total + plane[index].astype(F32)
    fin[:, 0:CA] = total.astype(BF)
    weight_grad()
    total = ts[block, rows_own, CA:WIDE].astype(F32)
    arrived(recv_z, R_Z)
    for index in range(7):
        total = total + recv_z[index].astype(F32)
    fin[:, CA:WIDE] = total.astype(BF)
    send(fin, fin_p, OUT_FIN, FIN, partner)
    weight_grad()
    arrived(fin_p, FIN)
    mine, theirs = fin[...].astype(F32), fin_p[...].astype(F32)
    whole = jnp.concatenate(
        [jnp.where(c == 0, mine, theirs), jnp.where(c == 0, theirs, mine)], axis=0
    )
    grad_x[...] = jnp.where(c == 0, whole[:, 0:PART], whole[:, PART:WIDE]).astype(BF)

    left(other_x, OUT_EX)
    left(kw.at[0 : 30 * UNIT], OUT_UNIT)
    left(x.at[:, 0 : 30 * UNIT, 0:CA], OUT_ROW)
    left(x.at[0, 0 : 14 * UNIT, 0:CB], OUT_TILE)
    left(x.at[:, 0 : 31 * UNIT, 0:CB], OUT_BLOCK)
    left(pair_w, OUT_W)
    left(grads_p, OUT_G)
    left(x.at[0:7, 0:256, 0:CA], OUT_SUM)
    left(x.at[0:4, 0 : 30 * UNIT, 0:CB], OUT_TERM)
    left(fin, OUT_FIN)


def store(*refs):
    sources, targets, sems = refs[:5], refs[5:10], refs[10]
    copies = [
        pltpu.make_async_copy(src, dst, sems.at[i])
        for i, (src, dst) in enumerate(zip(sources, targets))
    ]
    for copy in copies:
        copy.start()
    for copy in copies:
        copy.wait()


def per_device(encoder_states, queries, grad_context, key_weight, value_weight):
    anywhere = pl.BlockSpec(memory_space=pl.ANY)
    vmem = pl.BlockSpec(memory_space=pltpu.VMEM)
    shapes = ((1, TGT, 256), (1, TGT, 256), (1, D, 256), (1, D, 256), (32, PART))
    inputs = [
        pltpu.with_memory_space_constraint(array, pltpu.HBM)
        for array in (encoder_states, queries, grad_context, key_weight, value_weight)
    ]
    results = pl.pallas_call(
        kernel,
        out_shape=tuple(pltpu.VMEM(shape, BF) for shape in shapes),
        in_specs=[pl.BlockSpec(memory_space=pltpu.HBM)] * 5,
        out_specs=(vmem,) * 5,
        scratch_shapes=[
            pltpu.VMEM((8, SRC, WIDE), BF),
            pltpu.VMEM((D, 256), BF),
            pltpu.VMEM((D, 256), BF),
            pltpu.VMEM((2, D, 256), BF),
            pltpu.VMEM((UNIT, PART), BF),
            pltpu.VMEM((UNIT, PART), BF),
            pltpu.VMEM((TGT, 256), BF),
            pltpu.VMEM((TGT, 256), BF),
            pltpu.VMEM((SRC, 256), BF),
            pltpu.VMEM((SRC, 256), BF),
            pltpu.VMEM((SRC, 512), BF),
            pltpu.VMEM((HALF, 512), BF),
            pltpu.VMEM((8, HALF, WIDE), BF),
            pltpu.VMEM((4, 3, 128, CB), BF),
            pltpu.VMEM((3, 128, CB), BF),
            pltpu.VMEM((7, UNIT, CB), BF),
            pltpu.VMEM((32, 4, UNIT, CA), BF),
            pltpu.VMEM((15, UNIT, CA), BF),
            pltpu.VMEM((UNIT, WIDE), BF),
            pltpu.VMEM((UNIT, WIDE), BF),
            pltpu.SemaphoreType.DMA((SENDS,)),
            pltpu.SemaphoreType.DMA((RECEIVES,)),
            pltpu.SemaphoreType.DMA((5,)),
        ],
        compiler_params=pltpu.CompilerParams(
            collective_id=0, has_side_effects=True, vmem_limit_bytes=40 << 20
        ),
        cost_estimate=pl.CostEstimate(
            flops=8_500_000_000, bytes_accessed=11_000_000, transcendentals=262_144
        ),
        name="cross_attention_step",
    )(*inputs)
    results = [pltpu.with_memory_space_constraint(result, pltpu.VMEM) for result in results]
    return pl.pallas_call(
        store,
        out_shape=tuple(jax.ShapeDtypeStruct(shape, BF) for shape in shapes),
        in_specs=[vmem] * 5,
        out_specs=(anywhere,) * 5,
        scratch_shapes=[pltpu.SemaphoreType.DMA((5,))],
        compiler_params=pltpu.CompilerParams(vmem_limit_bytes=4 << 20),
        name="store_outputs",
    )(*results)


def solution(mesh):
    in_specs = (
        P("section", "tensor"),
        P("section", None, "tensor"),
        P("section", None, "tensor"),
        P("section", None, "tensor"),
        P("section", None, "tensor"),
    )
    out_specs = (
        P("section", None, "tensor"),
        P("section", None, "tensor"),
        P("section", None, "tensor"),
        P("section", None, "tensor"),
        P("section", "tensor"),
    )
    return jax.shard_map(
        per_device, mesh=mesh, in_specs=in_specs, out_specs=out_specs, check_vma=False
    )
```

```python
import functools

import jax
import jax.numpy as jnp
from jax import lax
from jax.experimental import pallas as pl
from jax.experimental.pallas import tpu as pltpu
from jax.sharding import PartitionSpec as P

MESH = pl.DeviceIdType.MESH
BF = jnp.bfloat16
F32 = jnp.float32

D = 5120
HS = 128
SRC = 512
TGT = 128
WIDE = 640
PART = WIDE // 2
CA = 256
CB = WIDE - CA
HALF = SRC // 2
UNIT = 16
SOFT_CAP = 20.0
SCALE = HS ** (-0.5)

EX = 0
A_PL = 1
A_Z = 5
B_Z = 19
B_P = 20
B_Q = 24
SHARE = 28
W_X = 29
G_X = 30
R_Q = 31
R_P = 35
R_Z = 36
S_Z = 37
S_PL = 51
FIN = 52
RECEIVES = 53

OUT_EX, OUT_UNIT, OUT_ROW, OUT_TILE, OUT_BLOCK, OUT_W, OUT_G, OUT_SUM, OUT_TERM, OUT_FIN = range(10)
SENDS = 10

GATHER_A = ((0, 0), (0, 1), (0, 3), (0, 2), (1, 0), (1, 1), (1, 3), (1, 2), (2, 0), (2, 1), (2, 3), (2, 2), (3, 0), (3, 1))
GATHER_B = ((0, 0), (0, 3), (0, 2), (0, 1), (1, 3), (1, 2), (1, 0), (1, 1), (2, 3), (2, 2), (2, 0), (2, 1), (3, 3), (3, 2))
RING_A = ((3, 0), (3, 1), (2, 2), (2, 3), (2, 0), (2, 1), (1, 2), (1, 3), (1, 0), (1, 1), (0, 2), (0, 3), (0, 0), (0, 1))
RING_B = ((2, 0), (3, 2), (3, 3), (2, 1), (2, 2), (2, 3), (1, 0), (1, 2), (1, 3), (1, 1), (0, 0), (0, 2), (0, 3), (0, 1))

NT = (((1,), (1,)), ((), ()))
TN = (((0,), (0,)), ((), ()))


def dot(a, b):
    return jnp.dot(a, b, preferred_element_type=F32)


def dot_nt(a, b):
    return lax.dot_general(a, b, NT, preferred_element_type=F32)


def dot_tn(a, b):
    return lax.dot_general(a, b, TN, preferred_element_type=F32)


def kernel(
    x_in, q_in, g_in, kw_in, vw_in,
    context, grad_q, grad_kw, grad_vw, grad_x,
    x, w, own_x, other_x, probs_held, raw_held, own_terms, qv, gv,
    keys, values, grads, grads_p, ts, recv_q, recv_p, recv_z, ring, plane, fin, fin_p,
    send_sem, recv_sem, local_sem,
):
    s = lax.axis_index("section")
    t = lax.axis_index("tensor")
    y_lo, z = lax.div(s, 8), lax.rem(s, 8)
    y_hi, c = lax.div(t, 8), lax.rem(t, 2)
    px = lax.rem(lax.div(t, 2), 4)
    py = y_hi * 2 + y_lo
    block = y_hi * 4 + px

    def at(xx, yy, zz, cc):
        return (lax.rem(yy, 2) * 8 + zz, lax.div(yy, 2) * 8 + xx * 2 + cc)

    def along(cc, dp, dq):
        dx = dp * cc + dq * (1 - cc)
        high = abs(dq) // 2 * cc + abs(dp) // 2 * (1 - cc)
        low = abs(dq) % 2 * cc + abs(dp) % 2 * (1 - cc)
        yy = (y_hi + high - 2 * y_hi * high) * 2 + y_lo + low - 2 * y_lo * low
        return lax.rem(px + dx + 4, 4), yy

    partner = at(px, py, z, 1 - c)

    def z_at(k):
        return lax.rem(z + k + 8, 8)

    def z_dev(k):
        return at(px, py, z_at(k), c)

    def rows16(cc, u, zz):
        return pl.ds(pl.multiple_of(cc * HALF + u * 128 + zz * UNIT, UNIT), UNIT)

    def remote(src, dst, out, slot, device):
        return pltpu.make_async_remote_copy(
            src_ref=src, dst_ref=dst, send_sem=send_sem.at[out], recv_sem=recv_sem.at[slot],
            device_id=device, device_id_type=MESH,
        )

    def send(src, dst, out, slot, device):
        remote(src, dst, out, slot, device).start()

    def arrived(dst, slot):
        remote(dst, dst, OUT_EX, slot, partner).wait_recv()

    def left(src, out):
        remote(src, src, out, EX, partner).wait_send()

    rows_own = pl.ds(pl.multiple_of(c * UNIT, UNIT), UNIT)
    rows_other = pl.ds(pl.multiple_of((1 - c) * UNIT, UNIT), UNIT)
    loads = [
        pltpu.make_async_copy(x_in, own_x, local_sem.at[0]),
        pltpu.make_async_copy(kw_in.at[0], w.at[:, 0:256], local_sem.at[1]),
        pltpu.make_async_copy(vw_in.at[0], w.at[:, 256:512], local_sem.at[2]),
        pltpu.make_async_copy(q_in.at[0], qv, local_sem.at[3]),
        pltpu.make_async_copy(g_in.at[0], gv, local_sem.at[4]),
    ]
    for load in loads:
        load.start()

    def row_of(m):
        return (1 - y_hi if m // 2 else y_hi), (1 - y_lo if m % 2 else y_lo)

    def in_plane(dx, m):
        high, low = row_of(m)
        return lax.rem(px + dx + 4, 4), high * 2 + low

    plane_offsets = [(dx, m) for m in (0, 1, 3, 2) for dx in (1, 3, 2, 0) if dx or m]

    barrier = pltpu.get_barrier_semaphore()
    peers = [partner] + [z_dev(k) for k in (1, 7, 2, 6, 3, 5, 4)]
    peers += [at(*in_plane(dx, m), z, c) for dx, m in plane_offsets]
    for peer in peers:
        pl.semaphore_signal(barrier, inc=1, device_id=peer, device_id_type=MESH)
    loads[0].wait()
    pl.semaphore_wait(barrier, len(peers))

    send(own_x.at[rows_other], other_x, OUT_EX, EX, partner)
    arrived(other_x, EX)
    mine, theirs = own_x[rows_own, :].astype(F32), other_x[...].astype(F32)
    first = jnp.where(c == 0, mine, theirs)
    second = jnp.where(c == 0, theirs, mine)
    x[block, rows16(c, y_lo, z), :] = jnp.concatenate([first, second], axis=1).astype(BF)

    def a_unit(ref, cc, place, zz):
        xx, yy = place
        return ref.at[lax.div(yy, 2) * 4 + xx, rows16(cc, lax.rem(yy, 2), zz), pl.ds(0, CA)]

    def a_row(ref, cc, m, zz):
        high, low = row_of(m)
        return ref.at[pl.ds(high * 4, 4), rows16(cc, low, zz), pl.ds(0, CA)]

    def b_unit(zz):
        return x.at[block, rows16(c, y_lo, zz), pl.ds(CA, CB)]

    def b_block(ref, cc, base, place):
        xx, yy = place
        rows = pl.ds(pl.multiple_of(base + lax.rem(yy, 2) * 128, 128), 128)
        return ref.at[lax.div(yy, 2) * 4 + xx, rows, pl.ds(CA, CB)]

    for dx, m in plane_offsets:
        unit = a_unit(x, c, (px, py), z)
        send(unit, unit, OUT_UNIT, A_PL + m, at(*in_plane(dx, m), z, c))
    for k in (1, 7, 2, 6, 3, 5, 4):
        send(b_unit(z), b_unit(z), OUT_TILE, B_Z, z_dev(k))

    loads[1].wait()
    loads[2].wait()
    for i in range(2):
        send(w.at[:, i * 256 : (i + 1) * 256], w.at[:, (i + 2) * 256 : (i + 3) * 256], OUT_W, W_X, partner)

    def share_a(k, m):
        part = a_row(x, c, m, z_at(k))
        send(part, part, OUT_ROW, SHARE, partner)

    def share_b(j, k):
        part = b_block(x, c, c * HALF, along(c, -j, -k))
        send(part, part, OUT_BLOCK, SHARE, partner)

    def spread_b(j):
        part = b_block(x, c, c * HALF, along(c, -j, 0))
        for k in (1, 3, 2):
            send(part, part, OUT_BLOCK, B_Q + j, at(*along(c, 0, k), z, c))
        share_b(j, 0)

    def pass_on(direction, step, m):
        sign = 1 - 2 * direction
        part = a_row(x, c, m, z_at(-sign * step))
        event = (GATHER_A, GATHER_B)[direction].index((step, m))
        send(part, part, OUT_ROW, A_Z + event, z_dev(sign))

    def ring_arrived(*events):
        for event in events:
            arrived(x.at[:, rows16(c, y_lo, z), pl.ds(0, CA)], A_Z + event)
            for direction, order in enumerate((GATHER_A, GATHER_B)):
                step, m = order[event]
                if step < 2 or (step == 2 and m // 2 == direction):
                    pass_on(direction, step + 1, m)
                share_a(-(1 - 2 * direction) * (step + 1), m)

    def ring_start(m):
        high, low = row_of(m)
        units = x.at[pl.ds(high * 4, 4 if m else 3), rows16(c, low, z), pl.ds(0, CA)]
        arrived(units, A_PL + m)
        pass_on(0, 0, m)
        pass_on(1, 0, m)
        share_a(0, m)

    ring_start(0)
    ring_start(1)
    arrived(x.at[block, pl.ds(0, 7 * UNIT), pl.ds(CA, CB)], B_Z)
    own_block = b_block(x, c, c * HALF, along(c, 0, 0))
    for k in (1, 3, 2):
        send(own_block, own_block, OUT_BLOCK, B_P + k, at(*along(c, k, 0), z, c))
    ring_start(3)
    ring_start(2)

    def block_arrived(j):
        arrived(b_block(x, c, c * HALF, along(c, -j, 0)), B_P + j)
        spread_b(j)

    def column_arrived(j):
        arrived(x.at[0:3, pl.ds(0, 128), pl.ds(CA, CB)], B_Q + j)
        for k in (1, 3, 2):
            share_b(j, k)

    ring_arrived(0)
    spread_b(0)
    ring_arrived(1)
    block_arrived(1)
    block_arrived(3)
    ring_arrived(2, 3)
    block_arrived(2)
    ring_arrived(4, 5)
    ring_arrived(6, 7)
    column_arrived(0)
    ring_arrived(8, 9)
    column_arrived(1)
    ring_arrived(10, 11)
    column_arrived(3)
    ring_arrived(12, 13)
    column_arrived(2)

    rows_c = pl.ds(pl.multiple_of(c * HALF, HALF), HALF)
    rows_p = pl.ds(pl.multiple_of((1 - c) * HALF, HALF), HALF)

    def project(rows):
        total = 0.0
        for i in range(4):
            wide = jnp.concatenate([x[2 * i, rows, :], x[2 * i + 1, rows, :]], axis=1)
            total += dot(wide, w[pl.ds(i * 2 * WIDE, 2 * WIDE), 0:512])
        keys[rows, :] = total[:, 0:256].astype(BF)
        values[rows, :] = total[:, 256:512].astype(BF)

    project(rows_c)
    arrived(x.at[:, rows_p, :], SHARE)
    project(rows_p)

    loads[3].wait()
    loads[4].wait()
    heads = [pl.ds(head * HS, HS) for head in range(2)]
    for head, cols in enumerate(heads):
        query, grad = qv[:, cols], gv[:, cols]
        key, value = keys[:, cols], values[:, cols]
        tangent = jnp.tanh(dot_nt(query, key) * SCALE / SOFT_CAP)
        weights = jnp.exp(SOFT_CAP * tangent)
        probs = weights / jnp.sum(weights, axis=-1, keepdims=True)
        probs_held[head] = probs.astype(BF)
        grad_probs = dot_nt(grad, value)
        inner = jnp.sum(probs * grad_probs, axis=-1, keepdims=True)
        grad_raw = probs * (grad_probs - inner) * (1.0 - tangent * tangent) * SCALE
        raw_held[head] = grad_raw.astype(BF)

    def key_value_grads(rows):
        for head, cols in enumerate(heads):
            grads[rows, cols] = dot_tn(raw_held[head, :, rows], qv[:, cols]).astype(BF)
            cols_v = pl.ds((2 + head) * HS, HS)
            grads[rows, cols_v] = dot_tn(probs_held[head, :, rows], gv[:, cols]).astype(BF)

    key_value_grads(rows_p)
    send(grads.at[rows_p], grads_p, OUT_G, G_X, partner)
    key_value_grads(rows_c)

    pieces = list(range(8))

    def weight_grad():
        i = pieces.pop(0)
        rows = pl.ds(i * WIDE, WIDE)
        both = dot_tn(x[i], grads[...]).astype(BF)
        grad_kw[0, rows, :] = both[:, 0:256]
        grad_vw[0, rows, :] = both[:, 256:512]

    for chip in range(8):
        own_terms[chip] = dot_nt(grads[rows_c, :], w[pl.ds(chip * WIDE, CA), 0:512])
    arrived(grads_p, G_X)
    arrived(w.at[:, 512:1024], W_X)

    def compute_a(half):
        high = row_of(half * 2)[0]
        for i in range(4):
            chip = high * 4 + i
            span = pl.ds(pl.multiple_of(chip * WIDE, 128), CA)
            ts[chip, :, 0:CA] = (own_terms[chip] + dot_nt(grads_p[...], w[span, 512:1024])).astype(BF)

    def scatter(direction, togo, m):
        sign = 1 - 2 * direction
        event = (RING_A, RING_B)[direction].index((togo - 1, m))
        part = a_row(ts, 0, m, z_at(sign * togo))
        send(part, ring.at[event, direction], OUT_SUM, S_Z + event, z_dev(sign))

    def ring_event(*events):
        for event in events:
            arrived(ring.at[event], S_Z + event)
            for direction, order in enumerate((RING_A, RING_B)):
                togo, m = order[event]
                high, low = row_of(m)
                chips, rows = pl.ds(high * 4, 4), rows16(0, low, z_at((1 - 2 * direction) * togo))
                total = ts[chips, rows, 0:CA].astype(F32) + ring[event, direction].astype(F32)
                ts[chips, rows, 0:CA] = total.astype(BF)
                if togo:
                    scatter(direction, togo, m)

    def send_b(j, k):
        send(
            b_block(ts, c, 0, along(c, j, k)), recv_q.at[j, k - 1],
            OUT_TERM, R_Q + j, at(*along(c, 0, k), z, c),
        )

    def compute_b(half):
        both = jnp.concatenate([grads[rows_c, :], grads_p[...]], axis=1)
        high = row_of(half * 2)[0]
        for i in range(4):
            chip = high * 4 + i
            span = pl.ds(pl.multiple_of(chip * WIDE + CA, 128), CB)
            ts[chip, :, CA:WIDE] = dot_nt(both, w[span, :]).astype(BF)

    def sum_b(j):
        xx, yy = along(c, j, 0)
        rows = pl.ds(pl.multiple_of(lax.rem(yy, 2) * 128, 128), 128)
        chip = lax.div(yy, 2) * 4 + xx
        total = ts[chip, rows, CA:WIDE].astype(F32)
        arrived(recv_q.at[j], R_Q + j)
        for k in range(3):
            total = total + recv_q[j, k].astype(F32)
        ts[chip, rows, CA:WIDE] = total.astype(BF)
        if j:
            part = b_block(ts, c, 0, along(c, j, 0))
            send(part, recv_p.at[j - 1], OUT_TERM, R_P, at(*along(c, j, 0), z, c))

    compute_a(0)
    for m in (0, 1):
        scatter(0, 4, m)
        scatter(1, 3, m)
    compute_a(1)
    for m in (2, 3):
        scatter(0, 3, m)
        scatter(1, 4, m)
    compute_b(1)

    @pl.when(c == 1)
    def _():
        for j in (3, 2, 1, 0):
            for k in (3, 2):
                send_b(j, k)

    @pl.when(c == 0)
    def _():
        for j in (3, 2):
            for k in (1, 3, 2):
                send_b(j, k)

    for head, cols in enumerate(heads):
        context[0, :, cols] = dot(probs_held[head], values[:, cols]).astype(BF)
        grad_q[0, :, cols] = dot(raw_held[head], keys[:, cols]).astype(BF)
    weight_grad()
    ring_event(0, 1)
    compute_b(0)

    @pl.when(c == 1)
    def _():
        for j in (3, 2, 1, 0):
            send_b(j, 1)

    @pl.when(c == 0)
    def _():
        for j in (1, 0):
            for k in (1, 3, 2):
                send_b(j, k)

    ring_event(2, 3)
    weight_grad()
    weight_grad()
    ring_event(4, 5)
    sum_b(3)
    ring_event(6, 7)
    sum_b(2)
    weight_grad()
    ring_event(8, 9)
    sum_b(1)
    ring_event(10, 11)
    sum_b(0)

    def send_plane(m):
        for dx in (2, 1, 3, 0):
            if dx or m:
                place = in_plane(dx, m)
                send(
                    a_unit(ts, 0, place, z), plane.at[m * 4 + dx - 1],
                    OUT_UNIT, S_PL, at(*place, z, c),
                )

    ring_event(12)
    send_plane(2)
    send_plane(0)
    ring_event(13)
    send_plane(3)
    send_plane(1)
    weight_grad()
    rows_b = pl.ds(pl.multiple_of(y_lo * 128, 128), 128)
    total = ts[block, rows_b, CA:WIDE].astype(F32)
    arrived(recv_p, R_P)
    for j in range(3):
        total = total + recv_p[j].astype(F32)
    ts[block, rows_b, CA:WIDE] = total.astype(BF)
    for k in (4, 3, 5, 2, 6, 1, 7):
        part = ts.at[block, rows16(0, y_lo, z_at(k)), pl.ds(CA, CB)]
        send(part, recv_z.at[k - 1], OUT_TILE, R_Z, z_dev(k))
    weight_grad()
    weight_grad()

    rows_own = rows16(0, y_lo, z)
    total = ts[block, rows_own, 0:CA].astype(F32)
    arrived(plane, S_PL)
    for index in range(15):
        total = total + plane[index].astype(F32)
    fin[:, 0:CA] = total.astype(BF)
    total = ts[block, rows_own, CA:WIDE].astype(F32)
    arrived(recv_z, R_Z)
    for index in range(7):
        total = total + recv_z[index].astype(F32)
    fin[:, CA:WIDE] = total.astype(BF)
    send(fin, fin_p, OUT_FIN, FIN, partner)
    weight_grad()
    arrived(fin_p, FIN)
    mine, theirs = fin[...].astype(F32), fin_p[...].astype(F32)
    whole = jnp.concatenate(
        [jnp.where(c == 0, mine, theirs), jnp.where(c == 0, theirs, mine)], axis=0
    )
    grad_x[...] = jnp.where(c == 0, whole[:, 0:PART], whole[:, PART:WIDE]).astype(BF)

    left(other_x, OUT_EX)
    left(w.at[0 : 30 * UNIT, 0:CA], OUT_UNIT)
    left(x.at[:, 0 : 30 * UNIT, 0:CA], OUT_ROW)
    left(x.at[0, 0 : 14 * UNIT, 0:CB], OUT_TILE)
    left(x.at[:, 0 : 31 * UNIT, 0:CB], OUT_BLOCK)
    left(w.at[:, 512:1024], OUT_W)
    left(grads_p, OUT_G)
    left(x.at[0:7, 0:256, 0:CA], OUT_SUM)
    left(x.at[0:4, 0 : 30 * UNIT, 0:CB], OUT_TERM)
    left(fin, OUT_FIN)


def store(*refs):
    sources, targets, sems = refs[:5], refs[5:10], refs[10]
    copies = [
        pltpu.make_async_copy(src, dst, sems.at[i])
        for i, (src, dst) in enumerate(zip(sources, targets))
    ]
    for copy in copies:
        copy.start()
    for copy in copies:
        copy.wait()


def per_device(encoder_states, queries, grad_context, key_weight, value_weight):
    anywhere = pl.BlockSpec(memory_space=pl.ANY)
    vmem = pl.BlockSpec(memory_space=pltpu.VMEM)
    shapes = ((1, TGT, 256), (1, TGT, 256), (1, D, 256), (1, D, 256), (32, PART))
    inputs = [
        pltpu.with_memory_space_constraint(array, pltpu.HBM)
        for array in (encoder_states, queries, grad_context, key_weight, value_weight)
    ]
    results = pl.pallas_call(
        kernel,
        out_shape=tuple(pltpu.VMEM(shape, BF) for shape in shapes),
        in_specs=[pl.BlockSpec(memory_space=pltpu.HBM)] * 5,
        out_specs=(vmem,) * 5,
        scratch_shapes=[
            pltpu.VMEM((8, SRC, WIDE), BF),
            pltpu.VMEM((D, 1024), BF),
            pltpu.VMEM((2 * UNIT, PART), BF),
            pltpu.VMEM((UNIT, PART), BF),
            pltpu.VMEM((2, TGT, SRC), BF),
            pltpu.VMEM((2, TGT, SRC), BF),
            pltpu.VMEM((8, HALF, CA), F32),
            pltpu.VMEM((TGT, 256), BF),
            pltpu.VMEM((TGT, 256), BF),
            pltpu.VMEM((SRC, 256), BF),
            pltpu.VMEM((SRC, 256), BF),
            pltpu.VMEM((SRC, 512), BF),
            pltpu.VMEM((HALF, 512), BF),
            pltpu.VMEM((8, HALF, WIDE), BF),
            pltpu.VMEM((4, 3, 128, CB), BF),
            pltpu.VMEM((3, 128, CB), BF),
            pltpu.VMEM((7, UNIT, CB), BF),
            pltpu.VMEM((14, 2, 4, UNIT, CA), BF),
            pltpu.VMEM((15, UNIT, CA), BF),
            pltpu.VMEM((UNIT, WIDE), BF),
            pltpu.VMEM((UNIT, WIDE), BF),
            pltpu.SemaphoreType.DMA((SENDS,)),
            pltpu.SemaphoreType.DMA((RECEIVES,)),
            pltpu.SemaphoreType.DMA((5,)),
        ],
        compiler_params=pltpu.CompilerParams(
            collective_id=0, has_side_effects=True, vmem_limit_bytes=40 << 20
        ),
        cost_estimate=pl.CostEstimate(
            flops=8_500_000_000, bytes_accessed=11_000_000, transcendentals=262_144
        ),
        name="cross_attention_step",
    )(*inputs)
    results = [pltpu.with_memory_space_constraint(result, pltpu.VMEM) for result in results]
    return pl.pallas_call(
        store,
        out_shape=tuple(jax.ShapeDtypeStruct(shape, BF) for shape in shapes),
        in_specs=[vmem] * 5,
        out_specs=(anywhere,) * 5,
        scratch_shapes=[pltpu.SemaphoreType.DMA((5,))],
        compiler_params=pltpu.CompilerParams(vmem_limit_bytes=4 << 20),
        name="store_outputs",
    )(*results)


def solution(mesh):
    in_specs = (
        P("section", "tensor"),
        P("section", None, "tensor"),
        P("section", None, "tensor"),
        P("section", None, "tensor"),
        P("section", None, "tensor"),
    )
    out_specs = (
        P("section", None, "tensor"),
        P("section", None, "tensor"),
        P("section", None, "tensor"),
        P("section", None, "tensor"),
        P("section", "tensor"),
    )
    return jax.shard_map(
        per_device, mesh=mesh, in_specs=in_specs, out_specs=out_specs, check_vma=False
    )
```

```python
import functools

import jax
import jax.numpy as jnp
from jax import lax
from jax.experimental import pallas as pl
from jax.experimental.pallas import tpu as pltpu
from jax.sharding import PartitionSpec as P

MESH = pl.DeviceIdType.MESH
BF = jnp.bfloat16
F32 = jnp.float32

D = 5120
HS = 128
SRC = 512
TGT = 128
WIDE = 640
PART = WIDE // 2
CA = 256
CB = WIDE - CA
UNIT = 32
SOFT_CAP = 20.0
SCALE = HS ** (-0.5)

EX, SHARE, W_X, G_X, FIN = range(5)
A_PL = 5
A_Z = 9
S_Z = 23
S_PL = 37
B_Z = 5
B_P = 6
B_Q = 14
R_Q = 22
R_P = 30
R_Z = 32
RECEIVES = 38

OUT_EX, OUT_W, OUT_G, OUT_FIN, OUT_1, OUT_2, OUT_3 = range(7)
SENDS = 7

GATHER_A = ((0, 0), (0, 1), (0, 3), (0, 2), (1, 0), (1, 1), (1, 3), (1, 2), (2, 0), (2, 1), (2, 3), (2, 2), (3, 0), (3, 1))
GATHER_B = ((0, 0), (0, 3), (0, 2), (0, 1), (1, 3), (1, 2), (1, 0), (1, 1), (2, 3), (2, 2), (2, 0), (2, 1), (3, 3), (3, 2))
RING_A = ((3, 0), (3, 1), (2, 2), (2, 3), (2, 0), (2, 1), (1, 2), (1, 3), (1, 0), (1, 1), (0, 2), (0, 3), (0, 0), (0, 1))
RING_B = ((2, 0), (3, 2), (3, 3), (2, 1), (2, 2), (2, 3), (1, 0), (1, 2), (1, 3), (1, 1), (0, 0), (0, 2), (0, 3), (0, 1))

NT = (((1,), (1,)), ((), ()))
TN = (((0,), (0,)), ((), ()))


def dot(a, b):
    return jnp.dot(a, b, preferred_element_type=F32)


def dot_nt(a, b):
    return lax.dot_general(a, b, NT, preferred_element_type=F32)


def dot_tn(a, b):
    return lax.dot_general(a, b, TN, preferred_element_type=F32)


def kernel(
    x_in, q_in, g_in, kw_in, vw_in,
    context, grad_q, grad_kw, grad_vw, grad_x,
    x, w, own_x, tail, tail_in, probs_held, raw_held, own_a, own_b, qv, gv,
    sums, grads, grads_p, ts_a, ts_b, recv_q, recv_p, recv_z, ring, plane, fin, fin_in,
    send_sem, recv_sem, local_sem,
):
    s = lax.axis_index("section")
    t = lax.axis_index("tensor")
    y_lo, z = lax.div(s, 8), lax.rem(s, 8)
    y_hi, c = lax.div(t, 8), lax.rem(t, 2)
    px = lax.rem(lax.div(t, 2), 4)
    block = y_hi * 4 + px

    def row_of(m):
        return (1 - y_hi if m // 2 else y_hi), (1 - y_lo if m % 2 else y_lo)

    def place(dx, m):
        return (lax.rem(px + dx + 4, 4),) + row_of(m)

    def at(where, zz, cc):
        xx, high, low = where
        return (low * 8 + zz, high * 8 + xx * 2 + cc)

    def along(h, dp, dq):
        return place(dp, abs(dq)) if h == 0 else place(dq, abs(dp))

    here = (px, y_hi, y_lo)
    partner = at(here, z, 1 - c)

    def z_at(k):
        return lax.rem(z + k + 8, 8)

    def rows_of(low, zz):
        first = low * 256 + lax.rem(zz, 2) * 128 + lax.div(zz, 2) * UNIT
        return pl.ds(pl.multiple_of(first, UNIT), UNIT)

    def remote(src, dst, out, slot, device):
        return pltpu.make_async_remote_copy(
            src_ref=src, dst_ref=dst, send_sem=send_sem.at[out], recv_sem=recv_sem.at[slot],
            device_id=device, device_id_type=MESH,
        )

    def send(src, dst, out, slot, device):
        remote(src, dst, out, slot, device).start()

    def arrived(dst, slot):
        remote(dst, dst, OUT_EX, slot, partner).wait_recv()

    def left(src, out):
        remote(src, src, out, EX, partner).wait_send()

    loads = [pltpu.make_async_copy(x_in, own_x, local_sem.at[0])]
    for head in range(2):
        for i, source in enumerate((kw_in, vw_in)):
            for chip in range(8):
                loads.append(
                    pltpu.make_async_copy(
                        source.at[0, chip * WIDE : (chip + 1) * WIDE, head * HS : (head + 1) * HS],
                        w.at[chip, :, (2 * head + i) * HS : (2 * head + i + 1) * HS],
                        local_sem.at[1],
                    )
                )
    loads.append(pltpu.make_async_copy(q_in.at[0], qv, local_sem.at[2]))
    loads.append(pltpu.make_async_copy(g_in.at[0], gv, local_sem.at[3]))
    for load in loads:
        load.start()

    plane_offsets = [(dx, m) for m in (0, 1, 3, 2) for dx in (1, 3, 2, 0) if dx or m]
    barrier = pltpu.get_barrier_semaphore()

    def greet(peers):
        for peer in peers:
            pl.semaphore_signal(barrier, inc=1, device_id=peer, device_id_type=MESH)
        pl.semaphore_wait(barrier, len(peers))

    @pl.when(c == 0)
    def _():
        greet(
            [partner, at(here, z_at(1), 0), at(here, z_at(-1), 0)]
            + [at(place(dx, m), z, 0) for dx, m in plane_offsets]
        )

    @pl.when(c == 1)
    def _():
        greet(
            [partner]
            + [at(here, z_at(k), 1) for k in (1, 7, 2, 6, 3, 5, 4)]
            + [at(place(dx, 0), z, 1) for dx in (1, 3, 2)]
            + [at(place(0, m), z, 1) for m in (1, 3, 2)]
        )

    loads[0].wait()
    own_rows = rows_of(y_lo, z)
    rows_a, rows_b = pl.ds(0, CA), pl.ds(CA, CB)

    def a_unit(ref, where, zz):
        xx, high, low = where
        return ref.at[high * 4 + xx, rows_of(low, zz), 0:CA]

    def a_row(ref, m, zz):
        high, low = row_of(m)
        return ref.at[pl.ds(high * 4, 4), rows_of(low, zz), 0:CA]

    def b_place(h, where):
        xx, high, low = where
        return high * 4 + xx, pl.ds(pl.multiple_of(low * 256 + h * 128, 128), 128)

    def weights_left():
        pltpu.make_async_copy(w.at[:, :, 0:512], w.at[:, :, 0:512], local_sem.at[1]).wait()

    @pl.when(c == 0)
    def _():
        spare = own_x[:, CA:PART].astype(F32)
        tail[...] = jnp.concatenate([spare, jnp.zeros_like(spare)], axis=1).astype(BF)
        send(tail, tail_in, OUT_EX, EX, partner)
        x[block, own_rows, 0:CA] = own_x[:, 0:CA]
        for dx, m in plane_offsets:
            unit = a_unit(x, here, z)
            send(unit, unit, OUT_1, A_PL + m, at(place(dx, m), z, 0))
        weights_left()
        send(w.at[:, rows_b, 0:512], w.at[:, rows_b, 512:1024], OUT_W, W_X, partner)

        def share(m, zz):
            part = a_row(x, m, zz)
            send(part, part, OUT_2, SHARE, partner)

        def pass_on(direction, step, m):
            sign = 1 - 2 * direction
            part = a_row(x, m, z_at(-sign * step))
            event = (GATHER_A, GATHER_B)[direction].index((step, m))
            send(part, part, OUT_2, A_Z + event, at(here, z_at(sign), 0))

        for m in (0, 1, 3, 2):
            high, low = row_of(m)
            units = x.at[pl.ds(high * 4, 4 if m else 3), rows_of(low, z), 0:CA]
            arrived(units, A_PL + m)
            pass_on(0, 0, m)
            pass_on(1, 0, m)
            share(m, z)
        for event in range(14):
            arrived(x.at[:, own_rows, 0:CA], A_Z + event)
            for direction, order in enumerate((GATHER_A, GATHER_B)):
                step, m = order[event]
                if step < 2 or (step == 2 and m // 2 == direction):
                    pass_on(direction, step + 1, m)
                share(m, z_at(-(1 - 2 * direction) * (step + 1)))

    @pl.when(c == 1)
    def _():
        arrived(tail_in, EX)
        spare, own = tail_in[...].astype(F32), own_x[...].astype(F32)
        x[block, own_rows, CA:WIDE] = jnp.concatenate([spare[:, 0 : PART - CA], own], axis=1).astype(BF)
        for k in (4, 3, 5, 2, 6, 1, 7):
            unit = x.at[block, own_rows, rows_b]
            send(unit, unit, OUT_1, B_Z, at(here, z_at(k), 1))
        weights_left()
        send(w.at[:, rows_a, 0:512], w.at[:, rows_a, 512:1024], OUT_W, W_X, partner)

        def part(h, dp, dq):
            chip, rows = b_place(h, along(h, dp, dq))
            return x.at[chip, rows, rows_b]

        def share(h, j, k):
            send(part(h, -j, -k), part(h, -j, -k), OUT_2, SHARE, partner)

        def spread(h, j):
            for k in (1, 3, 2):
                send(part(h, -j, 0), part(h, -j, 0), OUT_2, B_Q + h * 4 + j, at(along(h, 0, k), z, 1))
            share(h, j, 0)

        arrived(x.at[block, 0 : 7 * UNIT, rows_b], B_Z)
        for h in range(2):
            for k in (1, 3, 2):
                send(part(h, 0, 0), part(h, 0, 0), OUT_2, B_P + h * 4 + k, at(along(h, k, 0), z, 1))
        for h in range(2):
            spread(h, 0)
        for j in (1, 3, 2):
            for h in range(2):
                arrived(part(h, -j, 0), B_P + h * 4 + j)
                spread(h, j)
        for j in (0, 1, 3, 2):
            for h in range(2):
                arrived(x.at[0:3, 0:128, rows_b], B_Q + h * 4 + j)
                for k in (1, 3, 2):
                    share(h, j, k)

    def project(first, width, chips):
        wide = jnp.concatenate([x[i, :, first : first + width] for i in chips], axis=1)
        weights = jnp.concatenate([w[i, first : first + width, 0:512] for i in chips], axis=0)
        return dot(wide, weights)

    def project_all(first, width):
        return project(first, width, range(4)) + project(first, width, range(4, 8))

    @pl.when(c == 0)
    def _():
        sums[...] = project_all(0, CA)
        arrived(x.at[:, :, rows_b], SHARE)
        sums[...] += project_all(CA, CB)

    @pl.when(c == 1)
    def _():
        sums[...] = project_all(CA, CB)
        arrived(x.at[:, :, rows_a], SHARE)
        sums[...] += project_all(0, CA)

    loads[-2].wait()
    loads[-1].wait()
    heads = [pl.ds(head * HS, HS) for head in range(2)]

    def projected(head, i):
        first = (2 * head + i) * HS
        return sums[:, first : first + HS].astype(BF)

    for head, cols in enumerate(heads):
        query, grad = qv[:, cols], gv[:, cols]
        key, value = projected(head, 0), projected(head, 1)
        tangent = jnp.tanh(dot_nt(query, key) * SCALE / SOFT_CAP)
        weights = jnp.exp(SOFT_CAP * tangent)
        probs = weights / jnp.sum(weights, axis=-1, keepdims=True)
        probs_low = probs.astype(BF)
        probs_held[head] = probs_low
        grad_probs = dot_nt(grad, value)
        inner = jnp.sum(probs * grad_probs, axis=-1, keepdims=True)
        grad_raw = (probs * (grad_probs - inner) * (1.0 - tangent * tangent) * SCALE).astype(BF)
        raw_held[head] = grad_raw
        pair = pl.ds(head * 256, 256)
        grads[:, head * 256 : head * 256 + HS] = dot_tn(grad_raw, query).astype(BF)
        grads[:, head * 256 + HS : (head + 1) * 256] = dot_tn(probs_low, grad).astype(BF)
        send(grads.at[:, pair], grads_p.at[:, pair], OUT_G, G_X, partner)

    def small_outputs():
        for head, cols in enumerate(heads):
            context[0, :, cols] = dot(probs_held[head], projected(head, 1)).astype(BF)
            grad_q[0, :, cols] = dot(raw_held[head], projected(head, 0)).astype(BF)

    def weight_grad(*chips):
        for i in chips:
            rows = pl.ds(i * WIDE, WIDE)
            both = dot_tn(x[i], grads[...]).astype(BF)
            for head in range(2):
                grad_kw[0, rows, heads[head]] = both[:, head * 256 : head * 256 + HS]
                grad_vw[0, rows, heads[head]] = both[:, head * 256 + HS : (head + 1) * 256]

    @pl.when(c == 0)
    def _():
        for chip in range(8):
            own_a[chip] = dot_nt(grads[...], w[chip, rows_a, 0:512])
        arrived(grads_p, G_X)
        arrived(w.at[:, rows_a, 512:1024], W_X)

        def compute(half):
            high = row_of(half * 2)[0]
            for i in range(4):
                chip = high * 4 + i
                ts_a[chip] = (own_a[chip] + dot_nt(grads_p[...], w[chip, rows_a, 512:1024])).astype(BF)

        def scatter(direction, togo, m):
            sign = 1 - 2 * direction
            event = (RING_A, RING_B)[direction].index((togo - 1, m))
            source = a_row(ts_a, m, z_at(sign * togo))
            send(source, ring.at[event, direction], OUT_3, S_Z + event, at(here, z_at(sign), 0))

        def ring_event(*events):
            for event in events:
                arrived(ring.at[event], S_Z + event)
                for direction, order in enumerate((RING_A, RING_B)):
                    togo, m = order[event]
                    high, low = row_of(m)
                    chips, rows = pl.ds(high * 4, 4), rows_of(low, z_at((1 - 2 * direction) * togo))
                    total = ts_a[chips, rows, :].astype(F32) + ring[event, direction].astype(F32)
                    ts_a[chips, rows, :] = total.astype(BF)
                    if togo:
                        scatter(direction, togo, m)

        def send_plane(m):
            for dx in (2, 1, 3, 0):
                if dx or m:
                    where = place(dx, m)
                    send(a_unit(ts_a, where, z), plane.at[m * 4 + dx - 1], OUT_1, S_PL, at(where, z, 0))

        compute(0)
        for m in (0, 1):
            scatter(0, 4, m)
            scatter(1, 3, m)
        compute(1)
        for m in (2, 3):
            scatter(0, 3, m)
            scatter(1, 4, m)
        small_outputs()
        weight_grad(0)
        ring_event(0, 1)
        weight_grad(1)
        ring_event(2, 3)
        weight_grad(2)
        ring_event(4, 5)
        weight_grad(3)
        ring_event(6, 7)
        weight_grad(4)
        ring_event(8, 9)
        ring_event(10, 11, 12)
        send_plane(2)
        send_plane(0)
        ring_event(13)
        send_plane(3)
        send_plane(1)
        weight_grad(5, 6, 7)
        total = ts_a[block, own_rows, :].astype(F32)
        arrived(plane, S_PL)
        for index in range(15):
            total = total + plane[index].astype(F32)
        grad_x[:, 0:CA] = total.astype(BF)
        arrived(fin_in, FIN)
        grad_x[:, CA:PART] = fin_in[:, 0 : PART - CA]
        left(tail, OUT_EX)
        left(x.at[0:2, 0:480, 0:CA], OUT_1)
        left(w.at[:, rows_b, 0:512], OUT_W)
        left(x.at[:, 0:480, 0:512], OUT_2)
        left(x.at[0:7, :, 0:CA], OUT_3)

    @pl.when(c == 1)
    def _():
        def span(half):
            high = row_of(half * 2)[0]
            return [high * 4 + i for i in range(4)]

        for i, chip in enumerate(span(1)):
            own_b[i] = dot_nt(grads[...], w[chip, rows_b, 0:512])
        arrived(grads_p, G_X)
        arrived(w.at[:, rows_b, 512:1024], W_X)

        def send_q(h, j, k):
            chip, rows = b_place(h, along(h, j, k))
            send(
                ts_b.at[chip, rows], recv_q.at[h, j, k - 1],
                OUT_3, R_Q + h * 4 + j, at(along(h, 0, k), z, 1),
            )

        def sum_q(j):
            for h in range(2):
                chip, rows = b_place(h, along(h, j, 0))
                total = ts_b[chip, rows, :].astype(F32)
                arrived(recv_q.at[h, j], R_Q + h * 4 + j)
                for k in range(3):
                    total = total + recv_q[h, j, k].astype(F32)
                ts_b[chip, rows, :] = total.astype(BF)
                if j:
                    send(
                        ts_b.at[chip, rows], recv_p.at[h, j - 1],
                        OUT_3, R_P + h, at(along(h, j, 0), z, 1),
                    )

        for i, chip in enumerate(span(1)):
            ts_b[chip] = (own_b[i] + dot_nt(grads_p[...], w[chip, rows_b, 512:1024])).astype(BF)
        for j in (3, 2, 1, 0):
            for k in (3, 2):
                send_q(0, j, k)
            if j > 1:
                for k in (1, 3, 2):
                    send_q(1, j, k)
        both = jnp.concatenate([grads[...], grads_p[...]], axis=1)
        for chip in span(0):
            ts_b[chip] = dot_nt(both, w[chip, rows_b, :]).astype(BF)
        for j in (3, 2, 1, 0):
            send_q(0, j, 1)
            if j < 2:
                for k in (1, 3, 2):
                    send_q(1, j, k)
        small_outputs()
        weight_grad(0, 1, 2)
        sum_q(3)
        weight_grad(3)
        sum_q(2)
        weight_grad(4)
        sum_q(1)
        weight_grad(5)
        sum_q(0)
        for h in range(2):
            chip, rows = b_place(h, here)
            total = ts_b[chip, rows, :].astype(F32)
            arrived(recv_p.at[h], R_P + h)
            for j in range(3):
                total = total + recv_p[h, j].astype(F32)
            ts_b[chip, rows, :] = total.astype(BF)
        for k in (4, 3, 5, 2, 6, 1, 7):
            source = ts_b.at[block, rows_of(y_lo, z_at(k))]
            send(source, recv_z.at[k - 1], OUT_1, R_Z, at(here, z_at(k), 1))
        weight_grad(6, 7)
        total = ts_b[block, own_rows, :].astype(F32)
        arrived(recv_z, R_Z)
        for index in range(7):
            total = total + recv_z[index].astype(F32)
        fin[...] = total[:, 0:HS].astype(BF)
        send(fin, fin_in, OUT_FIN, FIN, partner)
        grad_x[...] = total[:, PART - CA : CB].astype(BF)
        left(x.at[0, 0 : 14 * UNIT, 0:CB], OUT_1)
        left(w.at[:, rows_a, 0:512], OUT_W)
        left(w.at[:, 0:496, 0:768], OUT_2)
        left(x.at[:, 0:480, 0:CB], OUT_3)
        left(fin, OUT_FIN)

    left(grads, OUT_G)


def store(*refs):
    sources, targets, sems = refs[:5], refs[5:10], refs[10]
    copies = [
        pltpu.make_async_copy(source, target, sems.at[i])
        for i, (source, target) in enumerate(zip(sources, targets))
    ]
    for copy in copies:
        copy.start()
    for copy in copies:
        copy.wait()


def per_device(encoder_states, queries, grad_context, key_weight, value_weight):
    anywhere = pl.BlockSpec(memory_space=pl.ANY)
    vmem = pl.BlockSpec(memory_space=pltpu.VMEM)
    shapes = ((1, TGT, 256), (1, TGT, 256), (1, D, 256), (1, D, 256), (32, PART))
    inputs = [
        pltpu.with_memory_space_constraint(array, pltpu.HBM)
        for array in (encoder_states, queries, grad_context, key_weight, value_weight)
    ]
    results = pl.pallas_call(
        kernel,
        out_shape=tuple(pltpu.VMEM(shape, BF) for shape in shapes),
        in_specs=[pl.BlockSpec(memory_space=pltpu.HBM)] * 5,
        out_specs=(vmem,) * 5,
        scratch_shapes=[
            pltpu.VMEM((8, SRC, WIDE), BF),
            pltpu.VMEM((8, WIDE, 1024), BF),
            pltpu.VMEM((UNIT, PART), BF),
            pltpu.VMEM((UNIT, HS), BF),
            pltpu.VMEM((UNIT, HS), BF),
            pltpu.VMEM((2, TGT, SRC), BF),
            pltpu.VMEM((2, TGT, SRC), BF),
            pltpu.VMEM((8, SRC, CA), F32),
            pltpu.VMEM((4, SRC, CB), F32),
            pltpu.VMEM((TGT, 256), BF),
            pltpu.VMEM((TGT, 256), BF),
            pltpu.VMEM((SRC, 512), F32),
            pltpu.VMEM((SRC, 512), BF),
            pltpu.VMEM((SRC, 512), BF),
            pltpu.VMEM((8, SRC, CA), BF),
            pltpu.VMEM((8, SRC, CB), BF),
            pltpu.VMEM((2, 4, 3, 128, CB), BF),
            pltpu.VMEM((2, 3, 128, CB), BF),
            pltpu.VMEM((7, UNIT, CB), BF),
            pltpu.VMEM((14, 2, 4, UNIT, CA), BF),
            pltpu.VMEM((15, UNIT, CA), BF),
            pltpu.VMEM((UNIT, HS), BF),
            pltpu.VMEM((UNIT, HS), BF),
            pltpu.SemaphoreType.DMA((SENDS,)),
            pltpu.SemaphoreType.DMA((RECEIVES,)),
            pltpu.SemaphoreType.DMA((4,)),
        ],
        compiler_params=pltpu.CompilerParams(
            collective_id=0, has_side_effects=True, vmem_limit_bytes=48 << 20
        ),
        cost_estimate=pl.CostEstimate(
            flops=8_500_000_000, bytes_accessed=11_000_000, transcendentals=262_144
        ),
        name="cross_attention_step",
    )(*inputs)
    results = [pltpu.with_memory_space_constraint(result, pltpu.VMEM) for result in results]
    return pl.pallas_call(
        store,
        out_shape=tuple(jax.ShapeDtypeStruct(shape, BF) for shape in shapes),
        in_specs=[vmem] * 5,
        out_specs=(anywhere,) * 5,
        scratch_shapes=[pltpu.SemaphoreType.DMA((5,))],
        compiler_params=pltpu.CompilerParams(vmem_limit_bytes=4 << 20),
        name="store_outputs",
    )(*results)


def solution(mesh):
    in_specs = (
        P("section", "tensor"),
        P("section", None, "tensor"),
        P("section", None, "tensor"),
        P("section", None, "tensor"),
        P("section", None, "tensor"),
    )
    out_specs = (
        P("section", None, "tensor"),
        P("section", None, "tensor"),
        P("section", None, "tensor"),
        P("section", None, "tensor"),
        P("section", "tensor"),
    )
    return jax.shard_map(
        per_device, mesh=mesh, in_specs=in_specs, out_specs=out_specs, check_vma=False
    )
```

```python
import functools

import jax
import jax.numpy as jnp
from jax import lax
from jax.experimental import pallas as pl
from jax.experimental.pallas import tpu as pltpu
from jax.sharding import PartitionSpec as P

MESH = pl.DeviceIdType.MESH
BF = jnp.bfloat16
F32 = jnp.float32

D = 5120
HS = 128
SRC = 512
TGT = 128
WIDE = 640
PART = WIDE // 2
CA = 256
CB = WIDE - CA
UNIT = 32
SOFT_CAP = 20.0
SCALE = HS ** (-0.5)

EX, SHARE, W_X, G_X, FIN = range(5)
A_PL = 5
A_Z = 9
S_Z = 23
S_PL = 37
B_Z = 5
B_P = 6
B_Q = 14
R_Q = 22
R_P = 30
R_Z = 32
RECEIVES = 38

OUT_EX, OUT_W, OUT_G, OUT_FIN, OUT_1, OUT_2, OUT_3 = range(7)
SENDS = 7

GATHER_A = ((0, 0), (0, 1), (0, 3), (0, 2), (1, 0), (1, 1), (1, 3), (1, 2), (2, 0), (2, 1), (2, 3), (2, 2), (3, 0), (3, 1))
GATHER_B = ((0, 0), (0, 1), (0, 3), (0, 2), (1, 0), (1, 1), (1, 3), (1, 2), (2, 0), (2, 1), (2, 3), (2, 2), (3, 3), (3, 2))
RING_A = ((3, 0), (3, 1), (2, 2), (2, 3), (2, 0), (2, 1), (1, 2), (1, 3), (1, 0), (1, 1), (0, 2), (0, 3), (0, 0), (0, 1))
RING_B = ((2, 0), (2, 1), (3, 2), (3, 3), (1, 0), (1, 1), (2, 2), (2, 3), (0, 0), (0, 1), (1, 2), (1, 3), (0, 2), (0, 3))

NT = (((1,), (1,)), ((), ()))
TN = (((0,), (0,)), ((), ()))


def dot(a, b):
    return jnp.dot(a, b, preferred_element_type=F32)


def dot_nt(a, b):
    return lax.dot_general(a, b, NT, preferred_element_type=F32)


def dot_tn(a, b):
    return lax.dot_general(a, b, TN, preferred_element_type=F32)


def kernel(
    x_in, q_in, g_in, kw_in, vw_in,
    context, grad_q, grad_kw, grad_vw, grad_x,
    x, w, own_x, tail, tail_in, probs_held, raw_held, own_a, own_b, qv, gv,
    sums, grads, grads_p, ts_a, ts_b, recv_q, recv_p, recv_z, ring, plane, fin, fin_in,
    send_sem, recv_sem, local_sem,
):
    s = lax.axis_index("section")
    t = lax.axis_index("tensor")
    y_lo, z = lax.div(s, 8), lax.rem(s, 8)
    y_hi, c = lax.div(t, 8), lax.rem(t, 2)
    px = lax.rem(lax.div(t, 2), 4)
    block = y_hi * 4 + px

    def row_of(m):
        return (1 - y_hi if m // 2 else y_hi), (1 - y_lo if m % 2 else y_lo)

    def place(dx, m):
        return (lax.rem(px + dx + 4, 4),) + row_of(m)

    def at(where, zz, cc):
        xx, high, low = where
        return (low * 8 + zz, high * 8 + xx * 2 + cc)

    def along(h, dp, dq):
        return place(dp, abs(dq)) if h == 0 else place(dq, abs(dp))

    here = (px, y_hi, y_lo)
    partner = at(here, z, 1 - c)

    def z_at(k):
        return lax.rem(z + k + 8, 8)

    def rows_of(low, zz):
        first = low * 256 + lax.rem(zz, 2) * 128 + lax.div(zz, 2) * UNIT
        return pl.ds(pl.multiple_of(first, UNIT), UNIT)

    def remote(src, dst, out, slot, device):
        return pltpu.make_async_remote_copy(
            src_ref=src, dst_ref=dst, send_sem=send_sem.at[out], recv_sem=recv_sem.at[slot],
            device_id=device, device_id_type=MESH,
        )

    def send(src, dst, out, slot, device):
        remote(src, dst, out, slot, device).start()

    def arrived(dst, slot):
        remote(dst, dst, OUT_EX, slot, partner).wait_recv()

    def left(src, out):
        remote(src, src, out, EX, partner).wait_send()

    loads = [pltpu.make_async_copy(x_in, own_x, local_sem.at[0])]
    for head in range(2):
        for i, source in enumerate((kw_in, vw_in)):
            for chip in range(8):
                loads.append(
                    pltpu.make_async_copy(
                        source.at[0, chip * WIDE : (chip + 1) * WIDE, head * HS : (head + 1) * HS],
                        w.at[chip, :, (2 * head + i) * HS : (2 * head + i + 1) * HS],
                        local_sem.at[1],
                    )
                )
    loads.append(pltpu.make_async_copy(q_in.at[0], qv, local_sem.at[2]))
    loads.append(pltpu.make_async_copy(g_in.at[0], gv, local_sem.at[3]))
    for load in loads:
        load.start()

    plane_offsets = [(dx, m) for m in (0, 1, 3, 2) for dx in (1, 3, 2, 0) if dx or m]
    barrier = pltpu.get_barrier_semaphore()

    def greet(peers):
        for peer in peers:
            pl.semaphore_signal(barrier, inc=1, device_id=peer, device_id_type=MESH)
        pl.semaphore_wait(barrier, len(peers))

    @pl.when(c == 0)
    def _():
        greet(
            [partner, at(here, z_at(1), 0), at(here, z_at(-1), 0)]
            + [at(place(dx, m), z, 0) for dx, m in plane_offsets]
        )

    @pl.when(c == 1)
    def _():
        greet(
            [partner]
            + [at(here, z_at(k), 1) for k in (1, 7, 2, 6, 3, 5, 4)]
            + [at(place(dx, 0), z, 1) for dx in (1, 3, 2)]
            + [at(place(0, m), z, 1) for m in (1, 3, 2)]
        )

    loads[0].wait()
    own_rows = rows_of(y_lo, z)
    rows_a, rows_b = pl.ds(0, CA), pl.ds(CA, CB)

    def a_unit(ref, where, zz):
        xx, high, low = where
        return ref.at[high * 4 + xx, rows_of(low, zz), 0:CA]

    def a_row(ref, m, zz):
        high, low = row_of(m)
        return ref.at[pl.ds(high * 4, 4), rows_of(low, zz), 0:CA]

    def b_place(h, where):
        xx, high, low = where
        return high * 4 + xx, pl.ds(pl.multiple_of(low * 256 + h * 128, 128), 128)

    def weights_left():
        pltpu.make_async_copy(w.at[:, :, 0:512], w.at[:, :, 0:512], local_sem.at[1]).wait()

    def project(first, width, chips, rows):
        wide = jnp.concatenate([x[i, rows, first : first + width] for i in chips], axis=1)
        weights = jnp.concatenate([w[i, first : first + width, 0:512] for i in chips], axis=0)
        return dot(wide, weights)

    def project_all(first, width, rows=slice(None)):
        return project(first, width, range(4), rows) + project(first, width, range(4, 8), rows)

    def project_parity(odd):
        for low in range(2):
            rows = pl.ds(pl.multiple_of(low * 256 + odd * 128, 128), 128)
            sums[rows, :] = project_all(0, CA, rows)

    @pl.when(c == 0)
    def _():
        spare = own_x[:, CA:PART].astype(F32)
        tail[...] = jnp.concatenate([spare, jnp.zeros_like(spare)], axis=1).astype(BF)
        send(tail, tail_in, OUT_EX, EX, partner)
        x[block, own_rows, 0:CA] = own_x[:, 0:CA]
        for dx, m in plane_offsets:
            unit = a_unit(x, here, z)
            send(unit, unit, OUT_1, A_PL + m, at(place(dx, m), z, 0))
        weights_left()
        send(w.at[:, rows_b, 0:512], w.at[:, rows_b, 512:1024], OUT_W, W_X, partner)

        def share(m, zz):
            part = a_row(x, m, zz)
            send(part, part, OUT_2, SHARE, partner)

        def pass_on(direction, step, m):
            sign = 1 - 2 * direction
            part = a_row(x, m, z_at(-sign * step))
            event = (GATHER_A, GATHER_B)[direction].index((step, m))
            send(part, part, OUT_2, A_Z + event, at(here, z_at(sign), 0))

        for m in (0, 1, 3, 2):
            high, low = row_of(m)
            units = x.at[pl.ds(high * 4, 4 if m else 3), rows_of(low, z), 0:CA]
            arrived(units, A_PL + m)
            pass_on(0, 0, m)
            pass_on(1, 0, m)
            share(m, z)
        def ring_arrived(*events):
            for event in events:
                arrived(x.at[:, own_rows, 0:CA], A_Z + event)
                pair = [order[event] for order in (GATHER_A, GATHER_B)]
                for direction, (step, m) in enumerate(pair):
                    if step < 2 or (step == 2 and m // 2 == direction):
                        pass_on(direction, step + 1, m)
                for direction, (step, m) in enumerate(pair):
                    share(m, z_at(-(1 - 2 * direction) * (step + 1)))

        ring_arrived(*range(12))
        project_parity(1 - lax.rem(z, 2))
        ring_arrived(12, 13)

    @pl.when(c == 1)
    def _():
        arrived(tail_in, EX)
        spare, own = tail_in[...].astype(F32), own_x[...].astype(F32)
        x[block, own_rows, CA:WIDE] = jnp.concatenate([spare[:, 0 : PART - CA], own], axis=1).astype(BF)
        for k in (4, 3, 5, 2, 6, 1, 7):
            unit = x.at[block, own_rows, rows_b]
            send(unit, unit, OUT_1, B_Z, at(here, z_at(k), 1))
        weights_left()
        send(w.at[:, rows_a, 0:512], w.at[:, rows_a, 512:1024], OUT_W, W_X, partner)

        def part(h, dp, dq):
            chip, rows = b_place(h, along(h, dp, dq))
            return x.at[chip, rows, rows_b]

        def share(h, j, k):
            send(part(h, -j, -k), part(h, -j, -k), OUT_2, SHARE, partner)

        def spread(h, j):
            for k in (1, 3, 2):
                send(part(h, -j, 0), part(h, -j, 0), OUT_2, B_Q + h * 4 + j, at(along(h, 0, k), z, 1))
            share(h, j, 0)

        arrived(x.at[block, 0 : 7 * UNIT, rows_b], B_Z)
        for h in range(2):
            for k in (1, 3, 2):
                send(part(h, 0, 0), part(h, 0, 0), OUT_2, B_P + h * 4 + k, at(along(h, k, 0), z, 1))
        for h in range(2):
            spread(h, 0)
        for j in (1, 3, 2):
            for h in range(2):
                arrived(part(h, -j, 0), B_P + h * 4 + j)
                spread(h, j)
        for j in (0, 1, 3, 2):
            for h in range(2):
                arrived(x.at[0:3, 0:128, rows_b], B_Q + h * 4 + j)
                for k in (1, 3, 2):
                    share(h, j, k)

    @pl.when(c == 0)
    def _():
        project_parity(lax.rem(z, 2))
        arrived(x.at[:, :, rows_b], SHARE)
        sums[...] += project_all(CA, CB)

    @pl.when(c == 1)
    def _():
        sums[...] = project_all(CA, CB)
        arrived(x.at[:, :, rows_a], SHARE)
        sums[...] += project_all(0, CA)

    loads[-2].wait()
    loads[-1].wait()
    heads = [pl.ds(head * HS, HS) for head in range(2)]

    def projected(head, i):
        first = (2 * head + i) * HS
        return sums[:, first : first + HS].astype(BF)

    for head, cols in enumerate(heads):
        query, grad = qv[:, cols], gv[:, cols]
        key, value = projected(head, 0), projected(head, 1)
        tangent = jnp.tanh(dot_nt(query, key) * SCALE / SOFT_CAP)
        weights = jnp.exp(SOFT_CAP * tangent)
        probs = weights / jnp.sum(weights, axis=-1, keepdims=True)
        probs_low = probs.astype(BF)
        probs_held[head] = probs_low
        grad_probs = dot_nt(grad, value)
        inner = jnp.sum(probs * grad_probs, axis=-1, keepdims=True)
        grad_raw = (probs * (grad_probs - inner) * (1.0 - tangent * tangent) * SCALE).astype(BF)
        raw_held[head] = grad_raw
        pair = pl.ds(head * 256, 256)
        grads[:, head * 256 : head * 256 + HS] = dot_tn(grad_raw, query).astype(BF)
        grads[:, head * 256 + HS : (head + 1) * 256] = dot_tn(probs_low, grad).astype(BF)
        send(grads.at[:, pair], grads_p.at[:, pair], OUT_G, G_X, partner)

    def small_outputs():
        for head, cols in enumerate(heads):
            context[0, :, cols] = dot(probs_held[head], projected(head, 1)).astype(BF)
            grad_q[0, :, cols] = dot(raw_held[head], projected(head, 0)).astype(BF)

    def weight_grad(*chips):
        for i in chips:
            rows = pl.ds(i * WIDE, WIDE)
            both = dot_tn(x[i], grads[...]).astype(BF)
            for head in range(2):
                grad_kw[0, rows, heads[head]] = both[:, head * 256 : head * 256 + HS]
                grad_vw[0, rows, heads[head]] = both[:, head * 256 + HS : (head + 1) * 256]

    @pl.when(c == 0)
    def _():
        for chip in range(8):
            own_a[chip] = dot_nt(grads[...], w[chip, rows_a, 0:512])
        arrived(grads_p, G_X)
        arrived(w.at[:, rows_a, 512:1024], W_X)

        def compute(half):
            high = row_of(half * 2)[0]
            for i in range(4):
                chip = high * 4 + i
                ts_a[chip] = (own_a[chip] + dot_nt(grads_p[...], w[chip, rows_a, 512:1024])).astype(BF)

        def scatter(direction, togo, m):
            sign = 1 - 2 * direction
            event = (RING_A, RING_B)[direction].index((togo - 1, m))
            source = a_row(ts_a, m, z_at(sign * togo))
            send(source, ring.at[event, direction], OUT_3, S_Z + event, at(here, z_at(sign), 0))

        def ring_event(*events):
            for event in events:
                arrived(ring.at[event], S_Z + event)
                for direction, order in enumerate((RING_A, RING_B)):
                    togo, m = order[event]
                    high, low = row_of(m)
                    chips, rows = pl.ds(high * 4, 4), rows_of(low, z_at((1 - 2 * direction) * togo))
                    total = ts_a[chips, rows, :].astype(F32) + ring[event, direction].astype(F32)
                    ts_a[chips, rows, :] = total.astype(BF)
                    if togo:
                        scatter(direction, togo, m)

        def send_plane(m):
            for dx in (2, 1, 3, 0):
                if dx or m:
                    where = place(dx, m)
                    send(a_unit(ts_a, where, z), plane.at[m * 4 + dx - 1], OUT_1, S_PL, at(where, z, 0))

        compute(0)
        for m in (0, 1):
            scatter(0, 4, m)
            scatter(1, 3, m)
        compute(1)
        for m in (2, 3):
            scatter(0, 3, m)
            scatter(1, 4, m)
        ring_event(0)
        ring_event(1)
        ring_event(2, 3)
        ring_event(4, 5)
        ring_event(6, 7)
        ring_event(8, 9)
        ring_event(10, 11)
        ring_event(12)
        send_plane(2)
        send_plane(0)
        ring_event(13)
        send_plane(3)
        send_plane(1)
        small_outputs()
        weight_grad(*range(8))
        total = ts_a[block, own_rows, :].astype(F32)
        arrived(plane, S_PL)
        for index in range(15):
            total = total + plane[index].astype(F32)
        grad_x[:, 0:CA] = total.astype(BF)
        arrived(fin_in, FIN)
        grad_x[:, CA:PART] = fin_in[:, 0 : PART - CA]
        left(tail, OUT_EX)
        left(x.at[0:2, 0:480, 0:CA], OUT_1)
        left(w.at[:, rows_b, 0:512], OUT_W)
        left(x.at[:, 0:480, 0:512], OUT_2)
        left(x.at[0:7, :, 0:CA], OUT_3)

    @pl.when(c == 1)
    def _():
        def span(half):
            high = row_of(half * 2)[0]
            return [high * 4 + i for i in range(4)]

        for i, chip in enumerate(span(1)):
            own_b[i] = dot_nt(grads[...], w[chip, rows_b, 0:512])
        arrived(grads_p, G_X)
        arrived(w.at[:, rows_b, 512:1024], W_X)

        def send_q(h, j, k):
            chip, rows = b_place(h, along(h, j, k))
            send(
                ts_b.at[chip, rows], recv_q.at[h, j, k - 1],
                OUT_3, R_Q + h * 4 + j, at(along(h, 0, k), z, 1),
            )

        def sum_q(j):
            for h in range(2):
                chip, rows = b_place(h, along(h, j, 0))
                total = ts_b[chip, rows, :].astype(F32)
                arrived(recv_q.at[h, j], R_Q + h * 4 + j)
                for k in range(3):
                    total = total + recv_q[h, j, k].astype(F32)
                ts_b[chip, rows, :] = total.astype(BF)
                if j:
                    send(
                        ts_b.at[chip, rows], recv_p.at[h, j - 1],
                        OUT_3, R_P + h, at(along(h, j, 0), z, 1),
                    )

        for i, chip in enumerate(span(1)):
            ts_b[chip] = (own_b[i] + dot_nt(grads_p[...], w[chip, rows_b, 512:1024])).astype(BF)
        for j in (3, 2, 1, 0):
            for k in (3, 2):
                send_q(0, j, k)
            if j > 1:
                for k in (1, 3, 2):
                    send_q(1, j, k)
        both = jnp.concatenate([grads[...], grads_p[...]], axis=1)
        for chip in span(0):
            ts_b[chip] = dot_nt(both, w[chip, rows_b, :]).astype(BF)
        for j in (3, 2, 1, 0):
            send_q(0, j, 1)
            if j < 2:
                for k in (1, 3, 2):
                    send_q(1, j, k)
        small_outputs()
        weight_grad(0, 1, 2)
        sum_q(3)
        weight_grad(3)
        sum_q(2)
        weight_grad(4)
        sum_q(1)
        weight_grad(5)
        sum_q(0)
        for h in range(2):
            chip, rows = b_place(h, here)
            total = ts_b[chip, rows, :].astype(F32)
            arrived(recv_p.at[h], R_P + h)
            for j in range(3):
                total = total + recv_p[h, j].astype(F32)
            ts_b[chip, rows, :] = total.astype(BF)
        for k in (4, 3, 5, 2, 6, 1, 7):
            source = ts_b.at[block, rows_of(y_lo, z_at(k))]
            send(source, recv_z.at[k - 1], OUT_1, R_Z, at(here, z_at(k), 1))
        weight_grad(6, 7)
        total = ts_b[block, own_rows, :].astype(F32)
        arrived(recv_z, R_Z)
        for index in range(7):
            total = total + recv_z[index].astype(F32)
        fin[...] = total[:, 0:HS].astype(BF)
        send(fin, fin_in, OUT_FIN, FIN, partner)
        grad_x[...] = total[:, PART - CA : CB].astype(BF)
        left(x.at[0, 0 : 14 * UNIT, 0:CB], OUT_1)
        left(w.at[:, rows_a, 0:512], OUT_W)
        left(w.at[:, 0:496, 0:768], OUT_2)
        left(x.at[:, 0:480, 0:CB], OUT_3)
        left(fin, OUT_FIN)

    left(grads, OUT_G)


def store(*refs):
    sources, targets, sems = refs[:5], refs[5:10], refs[10]
    copies = [
        pltpu.make_async_copy(source, target, sems.at[i])
        for i, (source, target) in enumerate(zip(sources, targets))
    ]
    for copy in copies:
        copy.start()
    for copy in copies:
        copy.wait()


def per_device(encoder_states, queries, grad_context, key_weight, value_weight):
    anywhere = pl.BlockSpec(memory_space=pl.ANY)
    vmem = pl.BlockSpec(memory_space=pltpu.VMEM)
    shapes = ((1, TGT, 256), (1, TGT, 256), (1, D, 256), (1, D, 256), (32, PART))
    inputs = [
        pltpu.with_memory_space_constraint(array, pltpu.HBM)
        for array in (encoder_states, queries, grad_context, key_weight, value_weight)
    ]
    results = pl.pallas_call(
        kernel,
        out_shape=tuple(pltpu.VMEM(shape, BF) for shape in shapes),
        in_specs=[pl.BlockSpec(memory_space=pltpu.HBM)] * 5,
        out_specs=(vmem,) * 5,
        scratch_shapes=[
            pltpu.VMEM((8, SRC, WIDE), BF),
            pltpu.VMEM((8, WIDE, 1024), BF),
            pltpu.VMEM((UNIT, PART), BF),
            pltpu.VMEM((UNIT, HS), BF),
            pltpu.VMEM((UNIT, HS), BF),
            pltpu.VMEM((2, TGT, SRC), BF),
            pltpu.VMEM((2, TGT, SRC), BF),
            pltpu.VMEM((8, SRC, CA), F32),
            pltpu.VMEM((4, SRC, CB), F32),
            pltpu.VMEM((TGT, 256), BF),
            pltpu.VMEM((TGT, 256), BF),
            pltpu.VMEM((SRC, 512), F32),
            pltpu.VMEM((SRC, 512), BF),
            pltpu.VMEM((SRC, 512), BF),
            pltpu.VMEM((8, SRC, CA), BF),
            pltpu.VMEM((8, SRC, CB), BF),
            pltpu.VMEM((2, 4, 3, 128, CB), BF),
            pltpu.VMEM((2, 3, 128, CB), BF),
            pltpu.VMEM((7, UNIT, CB), BF),
            pltpu.VMEM((14, 2, 4, UNIT, CA), BF),
            pltpu.VMEM((15, UNIT, CA), BF),
            pltpu.VMEM((UNIT, HS), BF),
            pltpu.VMEM((UNIT, HS), BF),
            pltpu.SemaphoreType.DMA((SENDS,)),
            pltpu.SemaphoreType.DMA((RECEIVES,)),
            pltpu.SemaphoreType.DMA((4,)),
        ],
        compiler_params=pltpu.CompilerParams(
            collective_id=0, has_side_effects=True, vmem_limit_bytes=48 << 20
        ),
        cost_estimate=pl.CostEstimate(
            flops=8_500_000_000, bytes_accessed=11_000_000, transcendentals=262_144
        ),
        name="cross_attention_step",
    )(*inputs)
    results = [pltpu.with_memory_space_constraint(result, pltpu.VMEM) for result in results]
    return pl.pallas_call(
        store,
        out_shape=tuple(jax.ShapeDtypeStruct(shape, BF) for shape in shapes),
        in_specs=[vmem] * 5,
        out_specs=(anywhere,) * 5,
        scratch_shapes=[pltpu.SemaphoreType.DMA((5,))],
        compiler_params=pltpu.CompilerParams(vmem_limit_bytes=4 << 20),
        name="store_outputs",
    )(*results)


def solution(mesh):
    in_specs = (
        P("section", "tensor"),
        P("section", None, "tensor"),
        P("section", None, "tensor"),
        P("section", None, "tensor"),
        P("section", None, "tensor"),
    )
    out_specs = (
        P("section", None, "tensor"),
        P("section", None, "tensor"),
        P("section", None, "tensor"),
        P("section", None, "tensor"),
        P("section", "tensor"),
    )
    return jax.shard_map(
        per_device, mesh=mesh, in_specs=in_specs, out_specs=out_specs, check_vma=False
    )
```
